128 devices in a mesh: visit: 32 (over y, x, core), patch: 4 (over z).
Axes of the slice: x: 4, y: 4, z: 4, core: 2. Of those that a mesh axis runs over, the one named last changes fastest.
Arguments:
- images: bfloat16 [32, 16, 512, 512], P('visit', 'patch'), may hold values from -6 to 6
- variances: bfloat16 [32, 16, 512, 512], P('visit', 'patch'), may hold values from 0.25 to 4
- kernels: bfloat16 [32, 2, 3, 31], P('visit'), may hold values from -1 to 1
- coefficients: bfloat16 [32, 16, 3, 3], P('visit', 'patch'), may hold values from -3 to 3
- intersections: int32 [32, 16, 2], P('visit', 'patch'), may hold values from 0 to 3, all different within a row; in each aligned block of 4 rows (0 to 3, 4 to 7, ..., all dimensions but the last counted through in order) at most 2 rows name the same one
- offsets: int32 [32, 16, 2, 2], P('visit', 'patch'), may hold values from 0 to 1024
Outputs:
- coadd: float32 [4, 1536, 1536], P('patch', 'visit')
- weight_map: float32 [4, 1536, 1536], P('patch', 'visit')
The draws below stay inside these ranges and needn't reach their ends.
Inputs may be any that keep to these rules, and one draw needn't show every extreme that they name: `intersections`: the two patches named for a tile differ. Among the 4 tiles that one device holds (aligned blocks of 4 CCDs of one visit) at most 2 name the same patch, a bound that some block reaches of them. `offsets`: every tile lies wholly inside each patch it intersects.
All inputs are finite; a program needn't handle non-finite values.
Results may differ from the reference program's by a relative error of at most 0.0065.
Values may be sent and summed in bfloat16 or wider, within the bound.
No kernel may reach another device: no remote copies, remote signals or barrier semaphores. Data moves between devices by JAX's collectives and lax.ppermute only.
A program may use at most 128 MiB of HBM per device.

```python
import math
import jax
import jax.numpy as jnp
import numpy as np
from jax import lax

TILE = 512
TAPS = 31
BASES = 3
PATCH_PIX = 1536
TILE_DEV = 4
CAP = 2
VISITS = 32
CCDS = 16
N_PATCH = 4


def place_ends(drawn, own_key, least, top_value):
    longest = drawn.shape.index(max(drawn.shape))
    spots = []
    for shift in (0, 1):
        where = [jax.random.randint(jax.random.fold_in(own_key, axis), (), 0, length) for axis, length in enumerate(drawn.shape)]
        where[longest] = (where[longest] + shift) % drawn.shape[longest]
        spots.append(tuple(where))
    return drawn.at[spots[0]].set(least).at[spots[1]].set(top_value)


def block_scale(rng, extent, cuts, smallest, top_value):
    loudness, own = 1.0, jax.random.fold_in(rng, 6)
    for dim, shards_of in cuts:
        steps = jnp.exp(jax.random.uniform(jax.random.fold_in(own, dim), (shards_of,), jnp.float32, smallest / len(cuts), top_value / len(cuts)))
        loudness = loudness * jnp.repeat(steps, extent[dim] // shards_of).reshape([-1 if axis == dim else 1 for axis in range(len(extent))])
    return loudness


def routed_block(rng, own, number, rows, count, top, reach, slope):
    order = jax.random.permutation(rng, count)
    heavy_load, common = load_shares(count, rows * top, reach, slope, True), load_shares(count, rows * top, reach, slope, False)
    places = jnp.arange(count)

    def named(tallies, rotation):
        used = int((tallies > 0).sum())
        fixed = max(1, used // 4)
        moved = fixed + (places - fixed + rotation * (used - fixed)) % max(1, count - fixed)
        return jnp.zeros((count,), jnp.int32).at[order[jnp.where(places < fixed, places, moved)]].set(jnp.asarray(tallies, jnp.int32))

    tallies = jnp.where(number % 4 == 0, named(heavy_load, number // 4), named(common, number - number // 4 - 1))
    mixed = jax.random.permutation(jax.random.fold_in(own, 3), count)
    giver, taker = mixed[0:count // 2 * 2:2], mixed[1:count // 2 * 2:2]
    room = jnp.minimum(tallies[giver] - 1, reach - tallies[taker]) // 2
    room = jnp.where((giver == order[0]) | (taker == order[0]) | (tallies[taker] == 0), 0, jnp.maximum(room, 0))
    moved = jax.random.randint(jax.random.fold_in(own, 4), (count // 2,), 0, 1 << 20) % (room + 1)
    tallies = tallies.at[giver].add(-moved).at[taker].add(moved)
    members = jnp.searchsorted(jnp.cumsum(tallies), jnp.arange(rows * top), side="right").astype(jnp.int32)
    grid = members.reshape(top, rows).T
    grid = grid[jax.random.permutation(jax.random.fold_in(own, 1), rows)]
    rotation = jax.random.randint(jax.random.fold_in(own, 2), (rows, 1), 0, top)
    return jnp.take_along_axis(grid, (jnp.arange(top)[None, :] + rotation) % top, axis=1)


def load_shares(number_of, total, most, lean, full):
    loads = [(1 << 20) // math.isqrt(rank ** lean) + 1 for rank in range(1, number_of + 1)]
    largest = most if full else min(most, max(-(-total // number_of), total * loads[0] // sum(loads)))
    least = 1 if total - largest >= number_of - 1 else 0
    given, spare = [largest] + [least] * (number_of - 1), total - largest - least * (number_of - 1)
    while spare > 0:
        free = [i for i in range(1, number_of) if given[i] < largest] or [i for i in range(1, number_of) if given[i] < most]
        mass, budget = sum([loads[i] for i in free]), spare
        for i in free:
            more = min(most - given[i], max(1, budget * loads[i] // mass), spare)
            given[i] = given[i] + more
            spare = spare - more
    return np.array(given)


def bell_draw(stream_key, dims, width, reach, shards=(), kind=jnp.bfloat16):
    values = jax.random.normal(stream_key, dims, jnp.float32) * width
    if len(shards) > 0:
        values = block_scale(stream_key, dims, shards, -0.22, 0.18) * values
    return jnp.clip(values, min=-reach, max=reach).astype(kind)


def setup_inputs(seed: int = 0) -> dict:
    arg_keys = jax.random.split(jax.random.key(seed), 7)
    images = bell_draw(arg_keys[0], (VISITS, CCDS, TILE, TILE), 1.0, 6.0, ((0, 32), (1, 4)))
    variances = jnp.clip(jnp.exp(math.log(4.0) - 2.7725887 * jax.random.uniform(arg_keys[1], (VISITS, CCDS, TILE, TILE), jnp.float32) ** block_scale(arg_keys[1], (VISITS, CCDS, TILE, TILE), ((0, 32), (1, 4)), -0.2, 0.2)), 0.25, 4.0).astype(jnp.bfloat16)
    kernels = bell_draw(arg_keys[2], (VISITS, 2, BASES, TAPS), 0.18, 1.0, ((0, 32),))
    coefficients = bell_draw(arg_keys[3], (VISITS, CCDS, BASES, 3), 0.6, 3.0, ((0, 32), (1, 4)))
    intersections_keys = jax.random.split(jax.random.fold_in(arg_keys[4], 1), VISITS * CCDS // TILE_DEV)
    intersections_turns = jax.random.permutation(jax.random.fold_in(arg_keys[4], 3), VISITS * CCDS // TILE_DEV)
    intersections = jax.vmap(lambda own, number: routed_block(jax.random.fold_in(arg_keys[4], 2), own, number, TILE_DEV, N_PATCH, 2, CAP, 2))(intersections_keys, intersections_turns).reshape((VISITS, CCDS, 2))
    offsets = place_ends(jax.random.randint(arg_keys[5], (VISITS, CCDS, 2, 2), 0, PATCH_PIX - TILE + 1), jax.random.fold_in(arg_keys[5], 1), 0, PATCH_PIX - TILE).astype(jnp.int32)
    return dict(images=images, variances=variances, kernels=kernels, coefficients=coefficients, intersections=intersections, offsets=offsets)


def band_table(taps, length):
    rowpos = jnp.arange(length, dtype=jnp.int32)[:, None]
    colpos = jnp.arange(length, dtype=jnp.int32)[None, :]
    spread = rowpos - colpos + (TAPS // 2)
    table = jnp.zeros((length, length), jnp.float32)
    for offset in range(TAPS):
        table = table + jnp.where(spread == offset, taps[offset].astype(jnp.float32), jnp.float32(0.0))
    return table.astype(jnp.bfloat16)


def match_image(image, coeffs, downs, acrosses):
    length = image.shape[0]
    coords = (jnp.arange(length, dtype=jnp.float32) - (length - 1) / 2.0) / (length / 2.0)
    total = jnp.zeros((length, length), jnp.float32)
    for basis in range(BASES):
        middle = jnp.dot(image, acrosses[basis], preferred_element_type=jnp.float32).astype(jnp.bfloat16)
        smoothed = lax.dot_general(downs[basis], middle, (((0,), (0,)), ((), ())), preferred_element_type=jnp.float32)
        factor = coeffs[basis].astype(jnp.float32)
        surface = factor[0] + factor[1] * coords[None, :] + factor[2] * coords[:, None]
        total = total + surface * smoothed
    return total.astype(jnp.bfloat16)


def reference(images, variances, kernels, coefficients, intersections, offsets):
    frame_shape = (N_PATCH, PATCH_PIX, PATCH_PIX)

    def visit_tile(index, carry):
        numer, denom = carry
        visit = index // CCDS
        ccd = index % CCDS
        kernel = kernels[visit]
        downs = [band_table(kernel[0, basis], TILE) for basis in range(BASES)]
        acrosses = [band_table(kernel[1, basis], TILE) for basis in range(BASES)]
        matched = match_image(images[visit, ccd], coefficients[visit, ccd], downs, acrosses).astype(jnp.float32)
        weight = 1.0 / variances[visit, ccd].astype(jnp.float32)
        weighted = weight * matched
        for which in range(2):
            start = (intersections[visit, ccd, which].astype(jnp.int32), offsets[visit, ccd, which, 0].astype(jnp.int32), offsets[visit, ccd, which, 1].astype(jnp.int32))
            region = lax.dynamic_slice(numer, start, (1, TILE, TILE))
            numer = lax.dynamic_update_slice(numer, region + weighted[None], start)
            region = lax.dynamic_slice(denom, start, (1, TILE, TILE))
            denom = lax.dynamic_update_slice(denom, region + weight[None], start)
        return numer, denom

    zeros = jnp.zeros(frame_shape, jnp.float32)
    numer, denom = lax.fori_loop(0, VISITS * CCDS, visit_tile, (zeros, zeros))
    return numer / (denom + 1.0), denom
```

```python
import functools

import jax
import jax.numpy as jnp
from jax import lax
from jax.experimental import pallas as pl
from jax.experimental.pallas import tpu as pltpu
from jax.sharding import PartitionSpec as P

TAPS = 31
BASES = 3
TILE = 512
PATCH_PIX = 1536
HALF = PATCH_PIX // 2
STRIP = 48
LANES = 128
ROWS = 8
SLAB = 384
BF16 = jnp.bfloat16
F32 = jnp.float32
BOTH = ("visit", "patch")


def visit_of(y, x, c):
    return (y * 4 + x) * 2 + c


def chips():
    return [(y, x) for y in range(4) for x in range(4)]


def across_x(value, step):
    pairs = [
        (visit_of(y, x, c), visit_of(y, (x + step) % 4, c)) for y, x in chips() for c in range(2)
    ]
    return lax.ppermute(value, "visit", pairs)


def across_y(value, step):
    pairs = [
        (visit_of(y, x, c), visit_of((y + step) % 4, x, c)) for y, x in chips() for c in range(2)
    ]
    return lax.ppermute(value, "visit", pairs)


def across_z(value, step):
    return lax.ppermute(value, "patch", [(z, (z + step) % 4) for z in range(4)])


def across_core(value):
    pairs = [(visit_of(y, x, c), visit_of(y, x, 1 - c)) for y, x in chips() for c in range(2)]
    return lax.ppermute(value, "visit", pairs)


def core_to_core(value, source, target, step):
    pairs = [
        (visit_of(y, x, source) * 4 + z, visit_of(y, x, target) * 4 + (z + step) % 4)
        for y, x in chips()
        for z in range(4)
    ]
    return lax.ppermute(value, BOTH, pairs)


def slot_of(info, entry):
    patch = info[0, entry]
    rank = jnp.int32(0)
    for other in range(8):
        rank += jnp.where((other < entry) & (info[0, other] == patch), 1, 0)
    return lax.rem(patch - info[0, 27] + 4, 4), jnp.minimum(rank, 1)


def weights_kernel(info, variance, plus, minus, held, sems):
    tile = pl.program_id(0)
    held[tile] = (1.0 / variance[0].astype(F32)).astype(BF16)

    def each(index, act):
        for which in range(2):
            towards, rank = slot_of(info, 2 * index + which)
            for wanted, target in ((1, plus), (3, minus)):

                @pl.when(towards == wanted)
                def _():
                    act(pltpu.make_async_copy(held.at[index], target.at[rank], sems.at[index, which]))

    each(tile, lambda copy: copy.start())

    @pl.when(tile == 3)
    def _():
        for index in range(4):
            each(index, lambda copy: copy.wait())


def send_weights(info, variances):
    out = jax.ShapeDtypeStruct((2, TILE, TILE), BF16)
    return pl.pallas_call(
        weights_kernel,
        grid=(4,),
        in_specs=[
            pl.BlockSpec(memory_space=pltpu.SMEM),
            pl.BlockSpec((1, TILE, TILE), lambda t: (t, 0, 0)),
        ],
        out_specs=[pl.BlockSpec(memory_space=pl.ANY)] * 2,
        out_shape=[out, out],
        scratch_shapes=[pltpu.VMEM((4, TILE, TILE), BF16), pltpu.SemaphoreType.DMA((4, 2))],
        compiler_params=pltpu.CompilerParams(vmem_limit_bytes=16 << 20),
        cost_estimate=pl.CostEstimate(flops=4 << 20, bytes_accessed=6 << 20, transcendentals=0),
    )(info, variances)


def match_kernel(
    info, coeffs, bands, image, variance, plus, minus, swap, stay, across, down, numer, weight, sems, wsems
):
    tile = pl.program_id(0)
    core = info[0, 26]

    @pl.when(tile == 0)
    def _():
        for basis in range(2 * BASES):
            row = jnp.broadcast_to(bands[basis : basis + 1, :], (LANES, 3 * LANES))
            band = pltpu.roll(row, 0, axis=1, stride=1, stride_axis=0).astype(BF16)
            table = across if basis < BASES else down
            for block in range(TILE // LANES):
                rows = slice(block * LANES, (block + 1) * LANES)
                table[basis % BASES, rows, :] = jnp.zeros((LANES, TILE), BF16)
                first = (block - 1) * LANES
                low, high = max(first, 0), min(first + 3 * LANES, TILE)
                table[basis % BASES, rows, low:high] = band[:, low - first : high - first]

    rows = lax.broadcasted_iota(jnp.int32, (TILE, 1), 0).astype(F32)
    columns = lax.broadcasted_iota(jnp.int32, (1, TILE), 1).astype(F32)
    rows = (rows - (TILE - 1) / 2.0) / (TILE / 2.0)
    columns = (columns - (TILE - 1) / 2.0) / (TILE / 2.0)
    total = jnp.zeros((TILE, TILE), F32)
    for basis in range(BASES):
        middle = jnp.dot(image[0], across[basis], preferred_element_type=F32).astype(BF16)
        smoothed = jnp.dot(down[basis], middle, preferred_element_type=F32)
        c0, c1, c2 = (coeffs[tile, 3 * basis + k] for k in range(3))
        total += ((c0 + c1 * columns) + c2 * rows) * smoothed
    inverse = 1.0 / variance[0].astype(F32)
    numer[tile] = (inverse * total).astype(BF16)
    weight[tile] = inverse.astype(BF16)

    def each(index, act):
        for which in range(2):
            towards, rank = slot_of(info, 2 * index + which)
            for wanted, target in ((1, plus), (3, minus)):

                @pl.when(towards == wanted)
                def _():
                    act(pltpu.make_async_copy(numer.at[index], target.at[rank], sems.at[index, which]))

            even = lax.rem(towards, 2) == 0
            place = lax.div(towards, 2)
            for own_core, (held, sent) in enumerate(((stay, swap), (swap, stay))):

                @pl.when(even & (core == own_core))
                def _():
                    act(pltpu.make_async_copy(numer.at[index], held.at[place, rank], sems.at[index, which]))
                    act(pltpu.make_async_copy(weight.at[index], sent.at[place, rank], wsems.at[index, which]))

    each(tile, lambda copy: copy.start())

    @pl.when(tile == 3)
    def _():
        for index in range(4):
            each(index, lambda copy: copy.wait())


def match_tiles(info, coeffs, bands, images, variances):
    pair = jax.ShapeDtypeStruct((2, TILE, TILE), BF16)
    quad = jax.ShapeDtypeStruct((2, 2, TILE, TILE), BF16)
    return pl.pallas_call(
        match_kernel,
        grid=(4,),
        in_specs=[
            pl.BlockSpec(memory_space=pltpu.SMEM),
            pl.BlockSpec(memory_space=pltpu.SMEM),
            pl.BlockSpec((8, 3 * LANES), lambda t: (0, 0)),
            pl.BlockSpec((1, TILE, TILE), lambda t: (t, 0, 0)),
            pl.BlockSpec((1, TILE, TILE), lambda t: (t, 0, 0)),
        ],
        out_specs=[pl.BlockSpec(memory_space=pl.ANY)] * 4,
        out_shape=[pair, pair, quad, quad],
        scratch_shapes=[
            pltpu.VMEM((BASES, TILE, TILE), BF16),
            pltpu.VMEM((BASES, TILE, TILE), BF16),
            pltpu.VMEM((4, TILE, TILE), BF16),
            pltpu.VMEM((4, TILE, TILE), BF16),
            pltpu.SemaphoreType.DMA((4, 2)),
            pltpu.SemaphoreType.DMA((4, 2)),
        ],
        compiler_params=pltpu.CompilerParams(vmem_limit_bytes=40 << 20),
        cost_estimate=pl.CostEstimate(flops=6 << 30, bytes_accessed=10 << 20, transcendentals=0),
    )(info, coeffs, bands, images, variances)


def frame_kernel(far, sources, table, *refs):
    stacks, refs = refs[: 2 if sources == 2 else 10], refs[2 if sources == 2 else 10 :]
    outs, (frame, held, packed, sems, out_sems) = refs[:8], refs[8:]
    y, x, core, z = (table[0, 24 + k] for k in range(4))
    patch = lax.rem(z + 2 * far, 4)

    def load(number):
        source, slot = number // 2, number % 2
        target, sem = held.at[number], sems.at[number]
        if source < 2:
            pltpu.make_async_copy(stacks[source].at[far, slot], target, sem).start()
            return
        for own_core in range(2):

            @pl.when(core == own_core)
            def _():
                stack = stacks[2 + 4 * own_core + source - 2]
                pltpu.make_async_copy(stack.at[slot], target, sem).start()

    for number in range(2 * sources):
        load(number)
    frame[...] = jnp.zeros_like(frame)
    apart = lax.broadcasted_iota(jnp.int32, (2 * LANES, LANES), 1) - lax.broadcasted_iota(
        jnp.int32, (2 * LANES, LANES), 0
    )

    inner = lax.broadcasted_iota(jnp.int32, (TILE // ROWS + 1, ROWS, LANES), 1)
    nothing = jnp.zeros((1, ROWS, LANES), F32)

    def add(number, carry):
        source, slot = lax.div(number, 2), lax.rem(number, 2)
        entry = jnp.int32(0)
        for k in range(8):
            named = table[source, k] == patch
            entry = jnp.where(named & ((slot == 1) | (entry == 0)), k + 1, entry)
        entry = jnp.maximum(entry - 1, 0)
        top, left = table[source, 8 + 2 * entry], table[source, 9 + 2 * entry]
        first = jnp.minimum(lax.div(left, LANES) * LANES, PATCH_PIX - TILE - LANES)
        group, lead = lax.div(top, ROWS), lax.rem(top, ROWS)
        shift = jnp.where(apart == left - first - LANES, F32(1.0), F32(0.0)).astype(BF16)
        pltpu.make_async_copy(stacks[0].at[far, 0], held.at[number], sems.at[number]).wait()
        for block in range(5):
            low, high = max(block - 1, 0) * LANES, min(block + 1, 4) * LANES
            moved = jnp.dot(
                held[number, :, low:high],
                shift[LANES * (block == 0) : 2 * LANES - LANES * (block == 4)],
                preferred_element_type=F32,
            )
            turned = pltpu.roll(moved.reshape(TILE // ROWS, ROWS, LANES), lead, axis=1)
            lower = jnp.concatenate([turned, nothing], axis=0)
            upper = jnp.concatenate([nothing, turned], axis=0)
            where = (
                pl.ds(group, TILE // ROWS + 1),
                slice(None),
                pl.ds(pl.multiple_of(first + block * LANES, LANES), LANES),
            )
            frame[where] += jnp.where(inner >= lead, lower, upper)
        return carry

    lax.fori_loop(0, 2 * sources, add, 0)

    copies = []
    for out in range(8):
        for part in range(4):
            dx, dy = (out, part) if out < 4 else (part, out - 4)
            for dc in range(2):
                row = (
                    2 * 4 * STRIP * lax.rem(y + dy, 4) + 2 * STRIP * lax.rem(x + dx, 4) + STRIP * lax.rem(core + dc, 2)
                )
                strip = frame[pl.ds(lax.div(row, ROWS), STRIP // ROWS), :, (out // 4) * HALF : (out // 4 + 1) * HALF]
                at = (2 * part + dc) * STRIP
                packed[out, at : at + STRIP, :] = strip.reshape(STRIP, HALF).astype(BF16)
        copies.append(pltpu.make_async_copy(packed.at[out], outs[out], out_sems.at[out]))
        copies[-1].start()
    for copy in copies:
        copy.wait()


def build_frame(far, sources, table, stacks):
    out = jax.ShapeDtypeStruct((SLAB, HALF), BF16)
    return pl.pallas_call(
        functools.partial(frame_kernel, far, sources),
        in_specs=[pl.BlockSpec(memory_space=pltpu.SMEM)] + [pl.BlockSpec(memory_space=pl.ANY)] * len(stacks),
        out_specs=[pl.BlockSpec(memory_space=pl.ANY)] * 8,
        out_shape=[out] * 8,
        scratch_shapes=[
            pltpu.VMEM((PATCH_PIX // ROWS + 1, ROWS, PATCH_PIX), F32),
            pltpu.VMEM((2 * sources, TILE, TILE), BF16),
            pltpu.VMEM((8, SLAB, HALF), BF16),
            pltpu.SemaphoreType.DMA((2 * sources,)),
            pltpu.SemaphoreType.DMA((8,)),
        ],
        compiler_params=pltpu.CompilerParams(vmem_limit_bytes=40 << 20),
        cost_estimate=pl.CostEstimate(flops=sources << 30, bytes_accessed=(5 + sources) << 20, transcendentals=0),
    )(table, *stacks)


def sum_kernel(count, *refs):
    for half in range(2):
        total = refs[half * count][...].astype(F32)
        for other in range(1, count):
            total += refs[half * count + other][...].astype(F32)
        for part in range(4):
            refs[2 * count + 4 * half + part][...] = total[part * 2 * STRIP : (part + 1) * 2 * STRIP].astype(BF16)


def sum_slabs(first, second):
    count = len(first)
    out = jax.ShapeDtypeStruct((2 * STRIP, HALF), BF16)
    return pl.pallas_call(
        functools.partial(sum_kernel, count),
        out_shape=[out] * 8,
        compiler_params=pltpu.CompilerParams(vmem_limit_bytes=40 << 20),
        cost_estimate=pl.CostEstimate(flops=6 << 20, bytes_accessed=(count + 1) << 20, transcendentals=0),
    )(*first, *second)


def spread(pieces, send):
    return [pieces[0]] + [send(pieces[step], step) for step in (1, 3, 2)]


def body(images, variances, kernels, coefficients, intersections, offsets):
    visit, z = lax.axis_index("visit"), lax.axis_index("patch")
    place = jnp.stack([visit // 8, (visit // 2) % 4, visit % 2, z]).astype(jnp.int32)
    info = jnp.concatenate([intersections.reshape(8), offsets.reshape(16), place, jnp.zeros((100,), jnp.int32)])
    info = info.reshape(1, LANES)

    weight_plus, weight_minus = send_weights(info, variances[0])
    weights = [
        core_to_core(buffer, source, 1, step)
        for source in range(2)
        for buffer, step in ((weight_plus, 1), (weight_minus, 3))
    ]
    chip = jnp.concatenate([info, across_core(info)])
    table = jnp.concatenate([chip, across_z(chip, 1), across_z(chip, 3)])

    taps = kernels[0].astype(F32)
    bands = jnp.concatenate([taps[1, :, ::-1], taps[0], jnp.zeros((2, TAPS), F32)])
    bands = jnp.pad(bands, ((0, 0), (LANES - TAPS // 2, 2 * LANES - TAPS + TAPS // 2)))
    coeffs = coefficients[0].astype(F32).reshape(4, 9)
    numer_plus, numer_minus, swap, stay = match_tiles(info, coeffs, bands, images[0], variances[0])
    swapped = across_core(swap)
    numers = [
        core_to_core(buffer, source, 0, step)
        for source in range(2)
        for buffer, step in ((numer_plus, 1), (numer_minus, 3))
    ]

    opposite = build_frame(1, 2, chip, [stay, swapped])
    first = spread(opposite[:4], across_x)
    second = spread(opposite[4:], across_y)
    passed = []
    for slabs in (first, second):
        total = sum(slab.astype(F32) for slab in slabs).astype(BF16)
        passed.append(across_z(total, 2))

    stacks = [stay, swapped, numers[0], numers[2], numers[1], numers[3], weights[2], weights[0], weights[3], weights[1]]
    own = build_frame(0, 6, table, stacks)
    first = spread(own[:4], across_x) + [passed[0]]
    second = spread(own[4:], across_y) + [passed[1]]
    pieces = sum_slabs(first, second)
    left = sum(piece.astype(F32) for piece in spread(pieces[:4], across_y))
    right = sum(piece.astype(F32) for piece in spread(pieces[4:], across_x))
    rows = jnp.concatenate([left, right], axis=1)
    keep, other = rows[:STRIP], across_core(rows[STRIP:])
    core = visit % 2
    numer = jnp.where(core == 0, keep, other)
    weight = jnp.where(core == 0, other, keep)
    return (numer / (weight + 1.0))[None], weight[None]


def solution(mesh):
    return jax.shard_map(
        body,
        mesh=mesh,
        in_specs=(
            P("visit", "patch", None, None),
            P("visit", "patch", None, None),
            P("visit", None, None, None),
            P("visit", "patch", None, None),
            P("visit", "patch", None),
            P("visit", "patch", None, None),
        ),
        out_specs=(P("patch", "visit", None), P("patch", "visit", None)),
        check_vma=False,
    )
```

```python
import functools

import jax
import jax.numpy as jnp
from jax import lax
from jax.experimental import pallas as pl
from jax.experimental.pallas import tpu as pltpu
from jax.sharding import PartitionSpec as P

TAPS = 31
BASES = 3
TILE = 512
PATCH_PIX = 1536
STRIP = 48
LANES = 128
ROWS = 8
SLAB = 384
BF16 = jnp.bfloat16
F32 = jnp.float32


def visit_of(y, x, c):
    return (y * 4 + x) * 2 + c


def chips():
    return [(y, x) for y in range(4) for x in range(4)]


def turn(value, step, second):
    pairs = []
    for y, x in chips():
        for c in range(2):
            along_y = (c == 1) != second
            target = visit_of((y + step) % 4, x, c) if along_y else visit_of(y, (x + step) % 4, c)
            pairs.append((visit_of(y, x, c), target))
    return lax.ppermute(value, "visit", pairs)


def across_z(value, step):
    return lax.ppermute(value, "patch", [(z, (z + step) % 4) for z in range(4)])


def across_core(value):
    pairs = [(visit_of(y, x, c), visit_of(y, x, 1 - c)) for y, x in chips() for c in range(2)]
    return lax.ppermute(value, "visit", pairs)


def across_both(value, step):
    pairs = [
        (visit_of(y, x, c) * 4 + z, visit_of(y, x, 1 - c) * 4 + (z + step) % 4)
        for y, x in chips()
        for c in range(2)
        for z in range(4)
    ]
    return lax.ppermute(value, ("visit", "patch"), pairs)


def info_kernel(patches, corners, info):
    for entry in range(8):
        tile, which = entry // 2, entry % 2
        info[0, entry] = patches[which, tile]
        info[0, 8 + 2 * entry] = corners[which, 0, tile]
        info[0, 9 + 2 * entry] = corners[which, 1, tile]


def pack_info(patches, corners):
    return pl.pallas_call(
        info_kernel,
        in_specs=[pl.BlockSpec(memory_space=pltpu.SMEM)] * 2,
        out_specs=pl.BlockSpec(memory_space=pltpu.SMEM),
        out_shape=jax.ShapeDtypeStruct((1, LANES), jnp.int32),
    )(patches, corners)


def match_kernel(
    place, patches, taps, coeffs, image, variance, stays, plus, minus, swaps, swap_plus, swap_minus,
    across, down, lanes, factors, numer, weight, sems, wsems,
):
    tile = pl.program_id(0)
    core, z = place[0, 2], place[0, 3]

    @pl.when(tile == 0)
    def _():
        lanes[...] = jnp.zeros_like(lanes)
        for basis in range(BASES):
            factors[basis, 0:4, 0:3] = coeffs[basis].astype(F32)
            for axis in range(2):
                lanes[2 * basis + axis : 2 * basis + axis + 1, 0:TAPS] = taps[basis, axis : axis + 1, :].astype(F32)
        for basis in range(BASES):
            for axis in range(2):
                row = jnp.broadcast_to(lanes[2 * basis + axis : 2 * basis + axis + 1, :], (LANES, 3 * LANES))
                band = pltpu.roll(row, LANES - TAPS // 2, axis=1, stride=1, stride_axis=0)
                if axis == 1:
                    band = band.T
                band = band.astype(BF16)
                table = across if axis == 1 else down
                table[basis] = jnp.zeros((TILE, TILE), BF16)
                for block in range(TILE // LANES):
                    first = (block - 1) * LANES
                    low, high = max(first, 0), min(first + 3 * LANES, TILE)
                    span = slice(block * LANES, (block + 1) * LANES)
                    if axis == 1:
                        table[basis, low:high, span] = band[low - first : high - first, :]
                    else:
                        table[basis, span, low:high] = band[:, low - first : high - first]

    rows = lax.broadcasted_iota(jnp.int32, (TILE, 1), 0).astype(F32)
    columns = lax.broadcasted_iota(jnp.int32, (1, TILE), 1).astype(F32)
    rows = (rows - (TILE - 1) / 2.0) / (TILE / 2.0)
    columns = (columns - (TILE - 1) / 2.0) / (TILE / 2.0)
    total = jnp.zeros((TILE, TILE), F32)
    for basis in range(BASES):
        middle = jnp.dot(image[0], across[basis], preferred_element_type=F32).astype(BF16)
        smoothed = jnp.dot(down[basis], middle, preferred_element_type=F32)
        c0, c1, c2 = (factors[basis, pl.ds(tile, 1), k : k + 1] for k in range(3))
        total += ((c0 + c1 * columns) + c2 * rows) * smoothed
    inverse = 1.0 / variance[0].astype(F32)
    numer[tile] = (inverse * total).astype(BF16)
    weight[tile] = inverse.astype(BF16)

    def each(index, act):
        for which in range(2):
            patch = patches[which, index]
            rank = jnp.int32(0)
            for other in range(8):
                before = (2 * index + which > other) & (patches[other % 2, other // 2] == patch)
                rank += jnp.where(before, 1, 0)
            rank = jnp.minimum(rank, 1)
            towards = lax.rem(patch - z + 4, 4)
            held, sent = numer.at[index], weight.at[index]
            sem, wsem = sems.at[index, which], wsems.at[index, which]
            for wanted, keep, give in (
                (0, stays.at[0], swaps.at[0]),
                (1, plus, swap_plus),
                (2, stays.at[1], swaps.at[1]),
                (3, minus, swap_minus),
            ):
                for own_core in range(2):

                    @pl.when((towards == wanted) & (core == own_core))
                    def _():
                        act(pltpu.make_async_copy(held, (give if own_core else keep).at[rank], sem))
                        act(pltpu.make_async_copy(sent, (keep if own_core else give).at[rank], wsem))

    each(tile, lambda copy: copy.start())

    @pl.when(tile == 3)
    def _():
        for index in range(4):
            each(index, lambda copy: copy.wait())


def match_tiles(place, patches, taps, coeffs, images, variances):
    pair = jax.ShapeDtypeStruct((2, TILE, TILE), BF16)
    quad = jax.ShapeDtypeStruct((2, 2, TILE, TILE), BF16)
    return pl.pallas_call(
        match_kernel,
        grid=(4,),
        in_specs=[
            pl.BlockSpec(memory_space=pltpu.SMEM),
            pl.BlockSpec(memory_space=pltpu.SMEM),
            pl.BlockSpec((BASES, 2, TAPS), lambda t: (0, 0, 0)),
            pl.BlockSpec((BASES, 4, 3), lambda t: (0, 0, 0)),
            pl.BlockSpec((1, TILE, TILE), lambda t: (t, 0, 0)),
            pl.BlockSpec((1, TILE, TILE), lambda t: (t, 0, 0)),
        ],
        out_specs=[pl.BlockSpec(memory_space=pl.ANY)] * 6,
        out_shape=[quad, pair, pair, quad, pair, pair],
        scratch_shapes=[
            pltpu.VMEM((BASES, TILE, TILE), BF16),
            pltpu.VMEM((BASES, TILE, TILE), BF16),
            pltpu.VMEM((8, 3 * LANES), F32),
            pltpu.VMEM((BASES, 8, LANES), F32),
            pltpu.VMEM((4, TILE, TILE), BF16),
            pltpu.VMEM((4, TILE, TILE), BF16),
            pltpu.SemaphoreType.DMA((4, 2)),
            pltpu.SemaphoreType.DMA((4, 2)),
        ],
        compiler_params=pltpu.CompilerParams(vmem_limit_bytes=40 << 20),
        cost_estimate=pl.CostEstimate(flops=6 << 30, bytes_accessed=12 << 20, transcendentals=0),
    )(place, patches, taps, coeffs, images, variances)


def frame_kernel(far, sources, place, mine, other, *refs):
    stacks, outs, (frame, held, packed, sems, out_sems) = refs[:sources], refs[sources : sources + 4], refs[sources + 4 :]
    y, x, core, z = (place[0, k] for k in range(4))
    patch = lax.rem(z + 2 * far, 4)

    for number in range(2 * sources):
        source, slot = number // 2, number % 2
        stack = stacks[source].at[far, slot] if source < 2 else stacks[source].at[slot]
        pltpu.make_async_copy(stack, held.at[number], sems.at[number]).start()
    frame[...] = jnp.zeros_like(frame)
    apart = lax.broadcasted_iota(jnp.int32, (2 * LANES, LANES), 1) - lax.broadcasted_iota(
        jnp.int32, (2 * LANES, LANES), 0
    )
    inner = lax.broadcasted_iota(jnp.int32, (TILE // ROWS + 1, ROWS, LANES), 1)
    nothing = jnp.zeros((1, ROWS, LANES), F32)

    def add(number, carry):
        source, slot = lax.div(number, 2), lax.rem(number, 2)
        sibling = lax.rem(source, 2) == 1
        from_z = lax.rem(z + jnp.where(source < 2, 4, jnp.where(source < 4, 3, 5)), 4)

        def look(k):
            return jnp.where(sibling, other[from_z, k], mine[from_z, k])

        entry = jnp.int32(0)
        for k in range(8):
            named = look(k) == patch
            entry = jnp.where(named & ((slot == 1) | (entry == 0)), k + 1, entry)
        entry = jnp.maximum(entry - 1, 0)
        top, left = look(8 + 2 * entry), look(9 + 2 * entry)
        first = jnp.minimum(lax.div(left, LANES) * LANES, PATCH_PIX - TILE - LANES)
        group, lead = lax.div(top, ROWS), lax.rem(top, ROWS)
        shift = jnp.where(apart == left - first - LANES, F32(1.0), F32(0.0)).astype(BF16)
        pltpu.make_async_copy(stacks[0].at[far, 0], held.at[number], sems.at[number]).wait()
        for block in range(5):
            low, high = max(block - 1, 0) * LANES, min(block + 1, 4) * LANES
            moved = jnp.dot(
                held[number, :, low:high],
                shift[LANES * (block == 0) : 2 * LANES - LANES * (block == 4)],
                preferred_element_type=F32,
            )
            turned = pltpu.roll(moved.reshape(TILE // ROWS, ROWS, LANES), lead, axis=1)
            lower = jnp.concatenate([turned, nothing], axis=0)
            upper = jnp.concatenate([nothing, turned], axis=0)
            where = (
                pl.ds(group, TILE // ROWS + 1),
                slice(None),
                pl.ds(pl.multiple_of(first + block * LANES, LANES), LANES),
            )
            frame[where] += jnp.where(inner >= lead, lower, upper)
        return carry

    lax.fori_loop(0, 2 * sources, add, 0)

    copies = []
    for out in range(4):
        for part in range(4):
            dx, dy = jnp.where(core == 0, out, part), jnp.where(core == 0, part, out)
            for dc in range(2):
                row = 8 * STRIP * lax.rem(y + dy, 4) + 2 * STRIP * lax.rem(x + dx, 4) + STRIP * lax.rem(core + dc, 2)
                strip = frame[pl.ds(lax.div(row, ROWS), STRIP // ROWS)]
                at = (2 * part + dc) * STRIP
                packed[out, at : at + STRIP, :] = strip.reshape(STRIP, PATCH_PIX).astype(BF16)
        copies.append(pltpu.make_async_copy(packed.at[out], outs[out], out_sems.at[out]))
        copies[-1].start()
    for copy in copies:
        copy.wait()


def build_frame(far, place, mine, other, stacks):
    sources = len(stacks)
    out = jax.ShapeDtypeStruct((SLAB, PATCH_PIX), BF16)
    return pl.pallas_call(
        functools.partial(frame_kernel, far, sources),
        in_specs=[pl.BlockSpec(memory_space=pltpu.SMEM)] * 3 + [pl.BlockSpec(memory_space=pl.ANY)] * sources,
        out_specs=[pl.BlockSpec(memory_space=pl.ANY)] * 4,
        out_shape=[out] * 4,
        scratch_shapes=[
            pltpu.VMEM((PATCH_PIX // ROWS + 1, ROWS, PATCH_PIX), F32),
            pltpu.VMEM((2 * sources, TILE, TILE), BF16),
            pltpu.VMEM((4, SLAB, PATCH_PIX), BF16),
            pltpu.SemaphoreType.DMA((2 * sources,)),
            pltpu.SemaphoreType.DMA((4,)),
        ],
        compiler_params=pltpu.CompilerParams(vmem_limit_bytes=40 << 20),
        cost_estimate=pl.CostEstimate(flops=sources << 30, bytes_accessed=(5 + sources) << 20, transcendentals=0),
    )(place, mine, other, *stacks)


def sum_kernel(count, *refs):
    for part in range(4):
        rows = slice(part * 2 * STRIP, (part + 1) * 2 * STRIP)
        total = refs[0][rows].astype(F32)
        for ref in refs[1:count]:
            total += ref[rows].astype(F32)
        refs[count + part][...] = total.astype(BF16)


def sum_slabs(slabs):
    count = len(slabs)
    out = jax.ShapeDtypeStruct((2 * STRIP, PATCH_PIX), BF16)
    return pl.pallas_call(
        functools.partial(sum_kernel, count),
        out_shape=[out] * 4,
        compiler_params=pltpu.CompilerParams(vmem_limit_bytes=40 << 20),
        cost_estimate=pl.CostEstimate(flops=3 << 20, bytes_accessed=(count + 1) << 20, transcendentals=0),
    )(*slabs)


def spread(pieces, second):
    return [pieces[0]] + [turn(pieces[step], step, second) for step in (1, 3, 2)]


def add_up(pieces):
    return sum(piece.astype(F32) for piece in pieces)


def body(images, variances, kernels, coefficients, intersections, offsets):
    visit, z = lax.axis_index("visit"), lax.axis_index("patch")
    core = lax.rem(visit, 2)
    place = jnp.stack([lax.div(visit, 8), lax.rem(lax.div(visit, 2), 4), core, z]).astype(jnp.int32).reshape(1, 4)
    patches = jnp.transpose(intersections[0])
    mine = lax.all_gather(pack_info(patches, jnp.transpose(offsets[0], (1, 2, 0))), "patch", axis=0, tiled=True)

    stays, plus, minus, swaps, swap_plus, swap_minus = match_tiles(
        place,
        patches,
        jnp.transpose(kernels[0], (1, 0, 2)),
        jnp.transpose(coefficients[0], (1, 0, 2)),
        images[0],
        variances[0],
    )
    swapped = across_core(swaps)
    other = across_core(mine)
    arrived = [across_z(plus, 1), across_both(swap_plus, 1), across_z(minus, 3), across_both(swap_minus, 3)]

    opposite = build_frame(1, place, mine, other, [stays, swapped])
    passed = across_z(add_up(spread(opposite, False)).astype(BF16), 2)
    own = build_frame(0, place, mine, other, [stays, swapped] + arrived)
    pieces = sum_slabs(spread(own, False) + [passed])
    rows = add_up(spread(pieces, True))
    keep, got = rows[:STRIP], across_core(rows[STRIP:])
    numer = jnp.where(core == 0, keep, got)
    weight = jnp.where(core == 0, got, keep)
    return (numer / (weight + 1.0))[None], weight[None]


def solution(mesh):
    return jax.shard_map(
        body,
        mesh=mesh,
        in_specs=(
            P("visit", "patch", None, None),
            P("visit", "patch", None, None),
            P("visit", None, None, None),
            P("visit", "patch", None, None),
            P("visit", "patch", None),
            P("visit", "patch", None, None),
        ),
        out_specs=(P("patch", "visit", None), P("patch", "visit", None)),
        check_vma=False,
    )
```

```python
import functools

import jax
import jax.numpy as jnp
from jax import lax
from jax.experimental import pallas as pl
from jax.experimental.pallas import tpu as pltpu
from jax.sharding import PartitionSpec as P

TAPS = 31
BASES = 3
TILE = 512
PATCH_PIX = 1536
STRIP = 48
LANES = 128
ROWS = 8
SLAB = 384
BF16 = jnp.bfloat16
F32 = jnp.float32


def visit_of(y, x, c):
    return (y * 4 + x) * 2 + c


def chips():
    return [(y, x) for y in range(4) for x in range(4)]


def turn(value, step, second):
    pairs = []
    for y, x in chips():
        for c in range(2):
            along_y = (c == 1) != second
            target = visit_of((y + step) % 4, x, c) if along_y else visit_of(y, (x + step) % 4, c)
            pairs.append((visit_of(y, x, c), target))
    return lax.ppermute(value, "visit", pairs)


def across_z(value, step):
    return lax.ppermute(value, "patch", [(z, (z + step) % 4) for z in range(4)])


def across_core(value):
    pairs = [(visit_of(y, x, c), visit_of(y, x, 1 - c)) for y, x in chips() for c in range(2)]
    return lax.ppermute(value, "visit", pairs)


def across_both(value, step):
    pairs = [
        (visit_of(y, x, c) * 4 + z, visit_of(y, x, 1 - c) * 4 + (z + step) % 4)
        for y, x in chips()
        for c in range(2)
        for z in range(4)
    ]
    return lax.ppermute(value, ("visit", "patch"), pairs)


def position():
    visit = lax.axis_index("visit")
    return lax.div(visit, 8), lax.rem(lax.div(visit, 2), 4), lax.rem(visit, 2), lax.axis_index("patch")


def lane_values(shape, pairs, default):
    lane = lax.broadcasted_iota(jnp.int32, shape, len(shape) - 1)
    out = jnp.full(shape, default, F32)
    for where, value in pairs:
        out = jnp.where(lane == where, value, out)
    return out


def match_kernel(
    patches_in, corners_in, taps_in, coeffs_in, image, variance, stays, plus, minus, swaps, swap_plus, swap_minus,
    patches, corners, taps, coeffs, across, down, lanes, factors, numer, weight, in_sems, sems, wsems,
):
    tile = pl.program_id(0)
    _, _, core, z = position()

    @pl.when(tile == 0)
    def _():
        small = [(patches_in, patches), (corners_in, corners), (taps_in, taps), (coeffs_in, coeffs)]
        copies = [pltpu.make_async_copy(a, b, in_sems.at[k]) for k, (a, b) in enumerate(small)]
        for copy in copies:
            copy.start()
        for copy in copies:
            copy.wait()
        lanes[...] = jnp.zeros_like(lanes)
        for basis in range(BASES):
            factors[basis, 0:4, 0:3] = coeffs[basis].astype(F32)
            for axis in range(2):
                lanes[2 * basis + axis : 2 * basis + axis + 1, 0:TAPS] = taps[basis, axis : axis + 1, :].astype(F32)
        for basis in range(BASES):
            for axis in range(2):
                row = jnp.broadcast_to(lanes[2 * basis + axis : 2 * basis + axis + 1, :], (LANES, 3 * LANES))
                band = pltpu.roll(row, LANES - TAPS // 2, axis=1, stride=1, stride_axis=0)
                if axis == 1:
                    band = band.T
                band = band.astype(BF16)
                table = across if axis == 1 else down
                table[basis] = jnp.zeros((TILE, TILE), BF16)
                for block in range(TILE // LANES):
                    first = (block - 1) * LANES
                    low, high = max(first, 0), min(first + 3 * LANES, TILE)
                    span = slice(block * LANES, (block + 1) * LANES)
                    if axis == 1:
                        table[basis, low:high, span] = band[low - first : high - first, :]
                    else:
                        table[basis, span, low:high] = band[:, low - first : high - first]

    rows = lax.broadcasted_iota(jnp.int32, (TILE, 1), 0).astype(F32)
    columns = lax.broadcasted_iota(jnp.int32, (1, TILE), 1).astype(F32)
    rows = (rows - (TILE - 1) / 2.0) / (TILE / 2.0)
    columns = (columns - (TILE - 1) / 2.0) / (TILE / 2.0)
    total = jnp.zeros((TILE, TILE), F32)
    for basis in range(BASES):
        middle = jnp.dot(image[0], across[basis], preferred_element_type=F32).astype(BF16)
        smoothed = jnp.dot(down[basis], middle, preferred_element_type=F32)
        c0, c1, c2 = (factors[basis, pl.ds(tile, 1), k : k + 1] for k in range(3))
        total += ((c0 + c1 * columns) + c2 * rows) * smoothed
    inverse = 1.0 / variance[0].astype(F32)
    numer[tile, 0:TILE] = (inverse * total).astype(BF16)
    weight[tile, 0:TILE] = inverse.astype(BF16)
    named, tops, lefts = [], [], []
    for which in range(2):
        patch = patches[which, tile].astype(F32)
        named += [(8 * which, patch), (8 * which + 1, patch)]
        for axis, parts in enumerate((tops, lefts)):
            corner = corners[which, axis, tile]
            fine = lax.rem(corner, 32)
            parts += [(8 * which, (corner - fine).astype(F32)), (8 * which + 1, fine.astype(F32))]
    for held in (numer, weight):
        for part, pairs in enumerate((named, tops, lefts)):
            note = lane_values((16, LANES), pairs, -1.0 if part == 0 else 0.0)
            held[tile, TILE : TILE + 16, part * LANES : (part + 1) * LANES] = note.astype(BF16)

    def each(index, act):
        for which in range(2):
            patch = patches[which, index]
            rank = jnp.int32(0)
            for other in range(8):
                before = (2 * index + which > other) & (patches[other % 2, other // 2] == patch)
                rank += jnp.where(before, 1, 0)
            rank = jnp.minimum(rank, 1)
            towards = lax.rem(patch - z + 4, 4)
            held, sent = numer.at[index], weight.at[index]
            sem, wsem = sems.at[index, which], wsems.at[index, which]
            for wanted, keep, give in (
                (0, stays.at[0], swaps.at[0]),
                (1, plus, swap_plus),
                (2, stays.at[1], swaps.at[1]),
                (3, minus, swap_minus),
            ):
                for own_core in range(2):

                    @pl.when((towards == wanted) & (core == own_core))
                    def _():
                        act(pltpu.make_async_copy(held, (give if own_core else keep).at[rank], sem))
                        act(pltpu.make_async_copy(sent, (keep if own_core else give).at[rank], wsem))

    each(tile, lambda copy: copy.start())

    @pl.when(tile == 3)
    def _():
        for index in range(4):
            each(index, lambda copy: copy.wait())


def match_tiles(patches, corners, taps, coeffs, images, variances):
    pair = jax.ShapeDtypeStruct((2, TILE + 16, TILE), BF16)
    quad = jax.ShapeDtypeStruct((2, 2, TILE + 16, TILE), BF16)
    return pl.pallas_call(
        match_kernel,
        grid=(4,),
        in_specs=[
            pl.BlockSpec(memory_space=pl.ANY),
            pl.BlockSpec(memory_space=pl.ANY),
            pl.BlockSpec(memory_space=pl.ANY),
            pl.BlockSpec(memory_space=pl.ANY),
            pl.BlockSpec((1, TILE, TILE), lambda t: (t, 0, 0)),
            pl.BlockSpec((1, TILE, TILE), lambda t: (t, 0, 0)),
        ],
        out_specs=[pl.BlockSpec(memory_space=pl.ANY)] * 6,
        out_shape=[quad, pair, pair, quad, pair, pair],
        scratch_shapes=[
            pltpu.SMEM((2, 4), jnp.int32),
            pltpu.SMEM((2, 2, 4), jnp.int32),
            pltpu.VMEM((BASES, 2, TAPS), BF16),
            pltpu.VMEM((BASES, 4, 3), BF16),
            pltpu.VMEM((BASES, TILE, TILE), BF16),
            pltpu.VMEM((BASES, TILE, TILE), BF16),
            pltpu.VMEM((8, 3 * LANES), F32),
            pltpu.VMEM((BASES, 8, LANES), F32),
            pltpu.VMEM((4, TILE + 16, TILE), BF16),
            pltpu.VMEM((4, TILE + 16, TILE), BF16),
            pltpu.SemaphoreType.DMA((4,)),
            pltpu.SemaphoreType.DMA((4, 2)),
            pltpu.SemaphoreType.DMA((4, 2)),
        ],
        compiler_params=pltpu.CompilerParams(vmem_limit_bytes=40 << 20),
        cost_estimate=pl.CostEstimate(flops=6 << 30, bytes_accessed=12 << 20, transcendentals=0),
    )(patches, corners, taps, coeffs, images, variances)


def frame_kernel(far, sources, *refs):
    stacks, outs, (frame, held, packed, sems, out_sems) = refs[:sources], refs[sources : sources + 4], refs[sources + 4 :]
    y, x, core, z = position()
    patch = lax.rem(z + 2 * far, 4).astype(F32)

    for number in range(2 * sources):
        source, slot = number // 2, number % 2
        stack = stacks[source].at[far, slot] if source < 2 else stacks[source].at[slot]
        pltpu.make_async_copy(stack, held.at[number], sems.at[number]).start()
    frame[...] = jnp.zeros_like(frame)
    apart = lax.broadcasted_iota(jnp.int32, (2 * LANES, LANES), 1) - lax.broadcasted_iota(
        jnp.int32, (2 * LANES, LANES), 0
    )
    inner = lax.broadcasted_iota(jnp.int32, (TILE // ROWS + 1, ROWS, LANES), 1)
    nothing = jnp.zeros((1, ROWS, LANES), F32)

    def add(number, carry):
        pltpu.make_async_copy(stacks[0].at[far, 0], held.at[number], sems.at[number]).wait()
        named, tops, lefts = (
            held[number, TILE : TILE + 16, part * LANES : (part + 1) * LANES].astype(F32)[0:1] for part in range(3)
        )
        top = jnp.sum(jnp.where(named == patch, tops, 0.0)).astype(jnp.int32)
        left = jnp.sum(jnp.where(named == patch, lefts, 0.0)).astype(jnp.int32)
        first = jnp.minimum(lax.div(left, LANES) * LANES, PATCH_PIX - TILE - LANES)
        group, lead = lax.div(top, ROWS), lax.rem(top, ROWS)
        shift = jnp.where(apart == left - first - LANES, F32(1.0), F32(0.0)).astype(BF16)
        for block in range(5):
            low, high = max(block - 1, 0) * LANES, min(block + 1, 4) * LANES
            moved = jnp.dot(
                held[number, 0:TILE, low:high],
                shift[LANES * (block == 0) : 2 * LANES - LANES * (block == 4)],
                preferred_element_type=F32,
            )
            turned = pltpu.roll(moved.reshape(TILE // ROWS, ROWS, LANES), lead, axis=1)
            lower = jnp.concatenate([turned, nothing], axis=0)
            upper = jnp.concatenate([nothing, turned], axis=0)
            where = (
                pl.ds(group, TILE // ROWS + 1),
                slice(None),
                pl.ds(pl.multiple_of(first + block * LANES, LANES), LANES),
            )
            frame[where] += jnp.where(inner >= lead, lower, upper)
        return carry

    lax.fori_loop(0, 2 * sources, add, 0)

    copies = []
    for out in range(4):
        for part in range(4):
            dx, dy = jnp.where(core == 0, out, part), jnp.where(core == 0, part, out)
            for dc in range(2):
                row = 8 * STRIP * lax.rem(y + dy, 4) + 2 * STRIP * lax.rem(x + dx, 4) + STRIP * lax.rem(core + dc, 2)
                strip = frame[pl.ds(lax.div(row, ROWS), STRIP // ROWS)]
                at = (2 * part + dc) * STRIP
                packed[out, at : at + STRIP, :] = strip.reshape(STRIP, PATCH_PIX).astype(BF16)
        copies.append(pltpu.make_async_copy(packed.at[out], outs[out], out_sems.at[out]))
        copies[-1].start()
    for copy in copies:
        copy.wait()


def build_frame(far, stacks):
    sources = len(stacks)
    out = jax.ShapeDtypeStruct((SLAB, PATCH_PIX), BF16)
    return pl.pallas_call(
        functools.partial(frame_kernel, far, sources),
        in_specs=[pl.BlockSpec(memory_space=pl.ANY)] * sources,
        out_specs=[pl.BlockSpec(memory_space=pl.ANY)] * 4,
        out_shape=[out] * 4,
        scratch_shapes=[
            pltpu.VMEM((PATCH_PIX // ROWS + 1, ROWS, PATCH_PIX), F32),
            pltpu.VMEM((2 * sources, TILE + 16, TILE), BF16),
            pltpu.VMEM((4, SLAB, PATCH_PIX), BF16),
            pltpu.SemaphoreType.DMA((2 * sources,)),
            pltpu.SemaphoreType.DMA((4,)),
        ],
        compiler_params=pltpu.CompilerParams(vmem_limit_bytes=40 << 20),
        cost_estimate=pl.CostEstimate(flops=sources << 30, bytes_accessed=(5 + sources) << 20, transcendentals=0),
    )(*stacks)


def sum_kernel(count, *refs):
    for part in range(4):
        rows = slice(part * 2 * STRIP, (part + 1) * 2 * STRIP)
        total = refs[0][rows].astype(F32)
        for ref in refs[1:count]:
            total += ref[rows].astype(F32)
        refs[count + part][...] = total.astype(BF16)


def sum_slabs(slabs):
    count = len(slabs)
    out = jax.ShapeDtypeStruct((2 * STRIP, PATCH_PIX), BF16)
    return pl.pallas_call(
        functools.partial(sum_kernel, count),
        out_shape=[out] * 4,
        compiler_params=pltpu.CompilerParams(vmem_limit_bytes=40 << 20),
        cost_estimate=pl.CostEstimate(flops=3 << 20, bytes_accessed=(count + 1) << 20, transcendentals=0),
    )(*slabs)


def spread(pieces, second):
    return [pieces[0]] + [turn(pieces[step], step, second) for step in (1, 3, 2)]


def add_up(pieces):
    return sum(piece.astype(F32) for piece in pieces)


def body(images, variances, kernels, coefficients, intersections, offsets):
    core = lax.rem(lax.axis_index("visit"), 2)
    stays, plus, minus, swaps, swap_plus, swap_minus = match_tiles(
        jnp.transpose(intersections[0]),
        jnp.transpose(offsets[0], (1, 2, 0)),
        jnp.transpose(kernels[0], (1, 0, 2)),
        jnp.transpose(coefficients[0], (1, 0, 2)),
        images[0],
        variances[0],
    )
    swapped = across_core(swaps)
    arrived = [across_z(plus, 1), across_both(swap_plus, 1), across_z(minus, 3), across_both(swap_minus, 3)]

    opposite = build_frame(1, [stays, swapped])
    passed = across_z(add_up(spread(opposite, False)).astype(BF16), 2)
    own = build_frame(0, [stays, swapped] + arrived)
    pieces = sum_slabs(spread(own, False) + [passed])
    rows = add_up(spread(pieces, True))
    keep, got = rows[:STRIP], across_core(rows[STRIP:])
    numer = jnp.where(core == 0, keep, got)
    weight = jnp.where(core == 0, got, keep)
    return (numer / (weight + 1.0))[None], weight[None]


def solution(mesh):
    return jax.shard_map(
        body,
        mesh=mesh,
        in_specs=(
            P("visit", "patch", None, None),
            P("visit", "patch", None, None),
            P("visit", None, None, None),
            P("visit", "patch", None, None),
            P("visit", "patch", None),
            P("visit", "patch", None, None),
        ),
        out_specs=(P("patch", "visit", None), P("patch", "visit", None)),
        check_vma=False,
    )
```

```python
import functools

import jax
import jax.numpy as jnp
from jax import lax
from jax.experimental import pallas as pl
from jax.experimental.pallas import tpu as pltpu
from jax.sharding import PartitionSpec as P

TAPS = 31
BASES = 3
TILE = 512
PATCH_PIX = 1536
STRIP = 48
LANES = 128
ROWS = 8
SLAB = 384
BF16 = jnp.bfloat16
F32 = jnp.float32


def visit_of(y, x, c):
    return (y * 4 + x) * 2 + c


def chips():
    return [(y, x) for y in range(4) for x in range(4)]


def turn(value, step, second):
    pairs = []
    for y, x in chips():
        for c in range(2):
            along_y = (c == 1) != second
            target = visit_of((y + step) % 4, x, c) if along_y else visit_of(y, (x + step) % 4, c)
            pairs.append((visit_of(y, x, c), target))
    return lax.ppermute(value, "visit", pairs)


def across_z(value, step):
    return lax.ppermute(value, "patch", [(z, (z + step) % 4) for z in range(4)])


def across_core(value):
    pairs = [(visit_of(y, x, c), visit_of(y, x, 1 - c)) for y, x in chips() for c in range(2)]
    return lax.ppermute(value, "visit", pairs)


def across_both(value, step):
    pairs = [
        (visit_of(y, x, c) * 4 + z, visit_of(y, x, 1 - c) * 4 + (z + step) % 4)
        for y, x in chips()
        for c in range(2)
        for z in range(4)
    ]
    return lax.ppermute(value, ("visit", "patch"), pairs)


def position():
    visit = lax.axis_index("visit")
    return lax.div(visit, 8), lax.rem(lax.div(visit, 2), 4), lax.rem(visit, 2), lax.axis_index("patch")


def lane_values(shape, pairs, default):
    lane = lax.broadcasted_iota(jnp.int32, shape, len(shape) - 1)
    out = jnp.full(shape, default, F32)
    for where, value in pairs:
        out = jnp.where(lane == where, value, out)
    return out


def match_kernel(
    patches_in, corners_in, taps_in, coeffs_in, image, variance, stays, plus, minus, swaps, swap_plus, swap_minus,
    patches, corners, taps, coeffs, across, down, lanes, factors, numer, weight, in_sems, sems, wsems,
):
    tile = pl.program_id(0)
    _, _, core, z = position()

    @pl.when(tile == 0)
    def _():
        small = [(patches_in, patches), (corners_in, corners), (taps_in, taps), (coeffs_in, coeffs)]
        copies = [pltpu.make_async_copy(a, b, in_sems.at[k]) for k, (a, b) in enumerate(small)]
        for copy in copies:
            copy.start()
        for copy in copies:
            copy.wait()
        lanes[...] = jnp.zeros_like(lanes)
        for basis in range(BASES):
            factors[basis, 0:4, 0:3] = coeffs[basis].astype(F32)
            for axis in range(2):
                lanes[2 * basis + axis : 2 * basis + axis + 1, 0:TAPS] = taps[basis, axis : axis + 1, :].astype(F32)
        for basis in range(BASES):
            for axis in range(2):
                row = jnp.broadcast_to(lanes[2 * basis + axis : 2 * basis + axis + 1, :], (LANES, 3 * LANES))
                band = pltpu.roll(row, LANES - TAPS // 2, axis=1, stride=1, stride_axis=0)
                if axis == 1:
                    band = band.T
                band = band.astype(BF16)
                table = across if axis == 1 else down
                table[basis] = jnp.zeros((TILE, TILE), BF16)
                for block in range(TILE // LANES):
                    first = (block - 1) * LANES
                    low, high = max(first, 0), min(first + 3 * LANES, TILE)
                    span = slice(block * LANES, (block + 1) * LANES)
                    if axis == 1:
                        table[basis, low:high, span] = band[low - first : high - first, :]
                    else:
                        table[basis, span, low:high] = band[:, low - first : high - first]

    rows = lax.broadcasted_iota(jnp.int32, (TILE, 1), 0).astype(F32)
    columns = lax.broadcasted_iota(jnp.int32, (1, TILE), 1).astype(F32)
    rows = (rows - (TILE - 1) / 2.0) / (TILE / 2.0)
    columns = (columns - (TILE - 1) / 2.0) / (TILE / 2.0)
    total = jnp.zeros((TILE, TILE), F32)
    for basis in range(BASES):
        middle = jnp.dot(image[0], across[basis], preferred_element_type=F32).astype(BF16)
        smoothed = jnp.dot(down[basis], middle, preferred_element_type=F32)
        c0, c1, c2 = (factors[basis, pl.ds(tile, 1), k : k + 1] for k in range(3))
        total += ((c0 + c1 * columns) + c2 * rows) * smoothed
    inverse = 1.0 / variance[0].astype(F32)
    numer[tile, 0:TILE] = (inverse * total).astype(BF16)
    weight[tile, 0:TILE] = inverse.astype(BF16)
    named, tops, lefts = [], [], []
    for which in range(2):
        patch = patches[which, tile].astype(F32)
        named += [(8 * which, patch), (8 * which + 1, patch)]
        for axis, parts in enumerate((tops, lefts)):
            corner = corners[which, axis, tile]
            fine = lax.rem(corner, 32)
            parts += [(8 * which, (corner - fine).astype(F32)), (8 * which + 1, fine.astype(F32))]
    for held in (numer, weight):
        for part, pairs in enumerate((named, tops, lefts)):
            note = lane_values((16, LANES), pairs, -1.0 if part == 0 else 0.0)
            held[tile, TILE : TILE + 16, part * LANES : (part + 1) * LANES] = note.astype(BF16)

    def each(index, act):
        for which in range(2):
            patch = patches[which, index]
            rank = jnp.int32(0)
            for other in range(8):
                before = (2 * index + which > other) & (patches[other % 2, other // 2] == patch)
                rank += jnp.where(before, 1, 0)
            rank = jnp.minimum(rank, 1)
            towards = lax.rem(patch - z + 4, 4)
            held, sent = numer.at[index], weight.at[index]
            sem, wsem = sems.at[index, which], wsems.at[index, which]
            for wanted, keep, give in (
                (0, stays.at[0], swaps.at[0]),
                (1, plus, swap_plus),
                (2, stays.at[1], swaps.at[1]),
                (3, minus, swap_minus),
            ):
                for own_core in range(2):

                    @pl.when((towards == wanted) & (core == own_core))
                    def _():
                        act(pltpu.make_async_copy(held, (give if own_core else keep).at[rank], sem))
                        act(pltpu.make_async_copy(sent, (keep if own_core else give).at[rank], wsem))

    each(tile, lambda copy: copy.start())

    @pl.when(tile == 3)
    def _():
        for index in range(4):
            each(index, lambda copy: copy.wait())


def match_tiles(patches, corners, taps, coeffs, images, variances):
    pair = jax.ShapeDtypeStruct((2, TILE + 16, TILE), BF16)
    quad = jax.ShapeDtypeStruct((2, 2, TILE + 16, TILE), BF16)
    return pl.pallas_call(
        match_kernel,
        grid=(4,),
        in_specs=[
            pl.BlockSpec(memory_space=pl.ANY),
            pl.BlockSpec(memory_space=pl.ANY),
            pl.BlockSpec(memory_space=pl.ANY),
            pl.BlockSpec(memory_space=pl.ANY),
            pl.BlockSpec((1, TILE, TILE), lambda t: (t, 0, 0)),
            pl.BlockSpec((1, TILE, TILE), lambda t: (t, 0, 0)),
        ],
        out_specs=[pl.BlockSpec(memory_space=pl.ANY)] * 6,
        out_shape=[quad, pair, pair, quad, pair, pair],
        scratch_shapes=[
            pltpu.SMEM((2, 4), jnp.int32),
            pltpu.SMEM((2, 2, 4), jnp.int32),
            pltpu.VMEM((BASES, 2, TAPS), BF16),
            pltpu.VMEM((BASES, 4, 3), BF16),
            pltpu.VMEM((BASES, TILE, TILE), BF16),
            pltpu.VMEM((BASES, TILE, TILE), BF16),
            pltpu.VMEM((8, 3 * LANES), F32),
            pltpu.VMEM((BASES, 8, LANES), F32),
            pltpu.VMEM((4, TILE + 16, TILE), BF16),
            pltpu.VMEM((4, TILE + 16, TILE), BF16),
            pltpu.SemaphoreType.DMA((4,)),
            pltpu.SemaphoreType.DMA((4, 2)),
            pltpu.SemaphoreType.DMA((4, 2)),
        ],
        compiler_params=pltpu.CompilerParams(vmem_limit_bytes=62 << 20),
        cost_estimate=pl.CostEstimate(flops=6 << 30, bytes_accessed=12 << 20, transcendentals=0),
    )(patches, corners, taps, coeffs, images, variances)


def frame_kernel(far, sources, *refs):
    stacks, outs, frame = refs[:sources], refs[-5:-1], refs[-1]
    y, x, core, z = position()
    patch = lax.rem(z + 2 * far, 4).astype(F32)
    frame[...] = jnp.zeros_like(frame)
    inner = lax.broadcasted_iota(jnp.int32, (1, ROWS, LANES), 1)
    lane = lax.broadcasted_iota(jnp.int32, (1, ROWS, LANES), 2)
    groups = TILE // ROWS

    def add(tile):
        named, tops, lefts = (
            tile[TILE : TILE + 16, part * LANES : (part + 1) * LANES].astype(F32)[0:1] for part in range(3)
        )
        top = jnp.sum(jnp.where(named == patch, tops, 0.0)).astype(jnp.int32)
        left = jnp.sum(jnp.where(named == patch, lefts, 0.0)).astype(jnp.int32)
        first = jnp.minimum(lax.div(left, LANES) * LANES, PATCH_PIX - TILE - LANES)
        shift = left - first
        group, lead = lax.div(top, ROWS), lax.rem(top, ROWS)
        before = jnp.zeros((groups, ROWS, LANES), F32)
        for block in range(5):
            turned = jnp.zeros((groups, ROWS, LANES), F32)
            if block < 4:
                part = tile[0:TILE, block * LANES : (block + 1) * LANES].astype(F32)
                turned = pltpu.roll(part, shift, axis=1).reshape(groups, ROWS, LANES)
                turned = pltpu.roll(turned, lead, axis=1)
            moved = jnp.where(lane >= shift, turned, before)
            before = turned
            nothing = jnp.zeros((1, ROWS, LANES), F32)
            lower = jnp.concatenate([moved, nothing], axis=0)
            upper = jnp.concatenate([nothing, moved], axis=0)
            where = (
                pl.ds(group, groups + 1),
                slice(None),
                pl.ds(pl.multiple_of(first + block * LANES, LANES), LANES),
            )
            frame[where] += jnp.where(inner >= lead, lower, upper)

    for source, stack in enumerate(stacks):

        def both(slot, carry, stack=stack, source=source):
            add(stack.at[far, slot] if source < 2 else stack.at[slot])
            return carry

        lax.fori_loop(0, 2, both, 0)

    for out in range(4):
        for part in range(4):
            dx, dy = jnp.where(core == 0, out, part), jnp.where(core == 0, part, out)
            for dc in range(2):
                row = 8 * STRIP * lax.rem(y + dy, 4) + 2 * STRIP * lax.rem(x + dx, 4) + STRIP * lax.rem(core + dc, 2)
                strip = frame[pl.ds(lax.div(row, ROWS), STRIP // ROWS)]
                at = (2 * part + dc) * STRIP
                outs[out][at : at + STRIP, :] = strip.reshape(STRIP, PATCH_PIX).astype(BF16)


def build_frame(far, stacks, after=()):
    sources = len(stacks)
    out = jax.ShapeDtypeStruct((SLAB, PATCH_PIX), BF16)
    return pl.pallas_call(
        functools.partial(frame_kernel, far, sources),
        in_specs=[pl.BlockSpec(memory_space=pltpu.VMEM)] * sources + [pl.BlockSpec(memory_space=pl.ANY)] * len(after),
        out_shape=[out] * 4,
        scratch_shapes=[pltpu.VMEM((PATCH_PIX // ROWS + 1, ROWS, PATCH_PIX), F32)],
        compiler_params=pltpu.CompilerParams(vmem_limit_bytes=40 << 20),
        cost_estimate=pl.CostEstimate(flops=sources << 30, bytes_accessed=(5 + sources) << 20, transcendentals=0),
    )(*stacks, *after)


def tie(value, *after):
    return pl.pallas_call(
        lambda *refs: None,
        in_specs=[pl.BlockSpec(memory_space=pl.ANY)] * (1 + len(after)),
        out_specs=pl.BlockSpec(memory_space=pl.ANY),
        out_shape=jax.ShapeDtypeStruct(value.shape, value.dtype),
        input_output_aliases={0: 0},
    )(value, *after)


def sum_kernel(count, *refs):
    for part in range(4):
        rows = slice(part * 2 * STRIP, (part + 1) * 2 * STRIP)
        total = refs[0][rows].astype(F32)
        for ref in refs[1:count]:
            total += ref[rows].astype(F32)
        refs[count + part][...] = total.astype(BF16)


def sum_slabs(slabs):
    count = len(slabs)
    out = jax.ShapeDtypeStruct((2 * STRIP, PATCH_PIX), BF16)
    return pl.pallas_call(
        functools.partial(sum_kernel, count),
        out_shape=[out] * 4,
        compiler_params=pltpu.CompilerParams(vmem_limit_bytes=40 << 20),
        cost_estimate=pl.CostEstimate(flops=3 << 20, bytes_accessed=(count + 1) << 20, transcendentals=0),
    )(*slabs)


def spread(pieces, second):
    return [pieces[0]] + [turn(pieces[step], step, second) for step in (1, 3, 2)]


def add_up(pieces):
    return sum(piece.astype(F32) for piece in pieces)


def body(images, variances, kernels, coefficients, intersections, offsets):
    core = lax.rem(lax.axis_index("visit"), 2)
    stays, plus, minus, swaps, swap_plus, swap_minus = match_tiles(
        jnp.transpose(intersections[0]),
        jnp.transpose(offsets[0], (1, 2, 0)),
        jnp.transpose(kernels[0], (1, 0, 2)),
        jnp.transpose(coefficients[0], (1, 0, 2)),
        images[0],
        variances[0],
    )
    swapped = across_core(swaps)
    below, above = across_z(plus, 1), across_z(minus, 3)
    opposite = build_frame(1, [stays, swapped])
    summed = add_up(spread(opposite, False)).astype(BF16)
    passed = across_z(summed, 2)
    below_too = across_both(tie(swap_plus, below, opposite[0]), 1)
    above_too = across_both(tie(swap_minus, above, opposite[0]), 3)
    own = build_frame(0, [stays, swapped, below, below_too, above, above_too], [summed])
    pieces = sum_slabs(spread(own, False) + [passed])
    rows = add_up(spread(pieces, True))
    keep, got = rows[:STRIP], across_core(rows[STRIP:])
    numer = jnp.where(core == 0, keep, got)
    weight = jnp.where(core == 0, got, keep)
    return (numer / (weight + 1.0))[None], weight[None]


def solution(mesh):
    return jax.shard_map(
        body,
        mesh=mesh,
        in_specs=(
            P("visit", "patch", None, None),
            P("visit", "patch", None, None),
            P("visit", None, None, None),
            P("visit", "patch", None, None),
            P("visit", "patch", None),
            P("visit", "patch", None, None),
        ),
        out_specs=(P("patch", "visit", None), P("patch", "visit", None)),
        check_vma=False,
    )
```

```python
import functools

import jax
import jax.numpy as jnp
from jax import lax
from jax.experimental import pallas as pl
from jax.experimental.pallas import tpu as pltpu
from jax.sharding import PartitionSpec as P

TAPS = 31
BASES = 3
TILE = 512
PATCH_PIX = 1536
STRIP = 48
LANES = 128
ROWS = 8
SLAB = 384
BF16 = jnp.bfloat16
F32 = jnp.float32


def visit_of(y, x, c):
    return (y * 4 + x) * 2 + c


def chips():
    return [(y, x) for y in range(4) for x in range(4)]


def turn(value, step, second):
    pairs = []
    for y, x in chips():
        for c in range(2):
            along_y = (c == 1) != second
            target = visit_of((y + step) % 4, x, c) if along_y else visit_of(y, (x + step) % 4, c)
            pairs.append((visit_of(y, x, c), target))
    return lax.ppermute(value, "visit", pairs)


def across_z(value, step):
    return lax.ppermute(value, "patch", [(z, (z + step) % 4) for z in range(4)])


def across_core(value):
    pairs = [(visit_of(y, x, c), visit_of(y, x, 1 - c)) for y, x in chips() for c in range(2)]
    return lax.ppermute(value, "visit", pairs)


def across_both(value, step):
    pairs = [
        (visit_of(y, x, c) * 4 + z, visit_of(y, x, 1 - c) * 4 + (z + step) % 4)
        for y, x in chips()
        for c in range(2)
        for z in range(4)
    ]
    return lax.ppermute(value, ("visit", "patch"), pairs)


def position():
    visit = lax.axis_index("visit")
    return lax.div(visit, 8), lax.rem(lax.div(visit, 2), 4), lax.rem(visit, 2), lax.axis_index("patch")


def lane_values(shape, pairs, default):
    lane = lax.broadcasted_iota(jnp.int32, shape, len(shape) - 1)
    out = jnp.full(shape, default, F32)
    for where, value in pairs:
        out = jnp.where(lane == where, value, out)
    return out


def match_kernel(
    patches_in, corners_in, taps_in, coeffs_in, images_in, variances_in, stays, plus, minus, swaps, swap_plus, swap_minus,
    patches, corners, taps, coeffs, images, variances, across, down, lanes, factors, numer, weight,
    in_sems, tile_sems, sems, wsems,
):
    tile = pl.program_id(0)
    loads = [
        [
            pltpu.make_async_copy(images_in.at[index], images.at[index], tile_sems.at[0, index]),
            pltpu.make_async_copy(variances_in.at[index], variances.at[index], tile_sems.at[1, index]),
        ]
        for index in (0, 1, 2, 3, tile)
    ]
    _, _, core, z = position()

    @pl.when(tile == 0)
    def _():
        small = [(patches_in, patches), (corners_in, corners), (taps_in, taps), (coeffs_in, coeffs)]
        copies = [pltpu.make_async_copy(a, b, in_sems.at[k]) for k, (a, b) in enumerate(small)]
        for copy in copies:
            copy.start()
        for pair in loads[:4]:
            for copy in pair:
                copy.start()
        for copy in copies:
            copy.wait()
        lanes[...] = jnp.zeros_like(lanes)
        for basis in range(BASES):
            factors[basis, 0:4, 0:3] = coeffs[basis].astype(F32)
            for axis in range(2):
                lanes[2 * basis + axis : 2 * basis + axis + 1, 0:TAPS] = taps[basis, axis : axis + 1, :].astype(F32)
        for basis in range(BASES):
            for axis in range(2):
                row = jnp.broadcast_to(lanes[2 * basis + axis : 2 * basis + axis + 1, :], (LANES, 3 * LANES))
                band = pltpu.roll(row, LANES - TAPS // 2, axis=1, stride=1, stride_axis=0)
                if axis == 1:
                    band = band.T
                band = band.astype(BF16)
                table = across if axis == 1 else down
                table[basis] = jnp.zeros((TILE, TILE), BF16)
                for block in range(TILE // LANES):
                    first = (block - 1) * LANES
                    low, high = max(first, 0), min(first + 3 * LANES, TILE)
                    span = slice(block * LANES, (block + 1) * LANES)
                    if axis == 1:
                        table[basis, low:high, span] = band[low - first : high - first, :]
                    else:
                        table[basis, span, low:high] = band[:, low - first : high - first]

    rows = lax.broadcasted_iota(jnp.int32, (TILE, 1), 0).astype(F32)
    columns = lax.broadcasted_iota(jnp.int32, (1, TILE), 1).astype(F32)
    rows = (rows - (TILE - 1) / 2.0) / (TILE / 2.0)
    columns = (columns - (TILE - 1) / 2.0) / (TILE / 2.0)
    for copy in loads[4]:
        copy.wait()
    total = jnp.zeros((TILE, TILE), F32)
    for basis in range(BASES):
        middle = jnp.dot(images[tile], across[basis], preferred_element_type=F32).astype(BF16)
        smoothed = jnp.dot(down[basis], middle, preferred_element_type=F32)
        c0, c1, c2 = (factors[basis, pl.ds(tile, 1), k : k + 1] for k in range(3))
        total += ((c0 + c1 * columns) + c2 * rows) * smoothed
    inverse = 1.0 / variances[tile].astype(F32)
    numer[tile, 0:TILE] = (inverse * total).astype(BF16)
    weight[tile, 0:TILE] = inverse.astype(BF16)
    named, tops, lefts = [], [], []
    for which in range(2):
        patch = patches[which, tile].astype(F32)
        named += [(8 * which, patch), (8 * which + 1, patch)]
        for axis, parts in enumerate((tops, lefts)):
            corner = corners[which, axis, tile]
            fine = lax.rem(corner, 32)
            parts += [(8 * which, (corner - fine).astype(F32)), (8 * which + 1, fine.astype(F32))]
    for held in (numer, weight):
        for part, pairs in enumerate((named, tops, lefts)):
            note = lane_values((16, LANES), pairs, -1.0 if part == 0 else 0.0)
            held[tile, TILE : TILE + 16, part * LANES : (part + 1) * LANES] = note.astype(BF16)

    def each(index, act):
        for which in range(2):
            patch = patches[which, index]
            rank = jnp.int32(0)
            for other in range(8):
                before = (2 * index + which > other) & (patches[other % 2, other // 2] == patch)
                rank += jnp.where(before, 1, 0)
            rank = jnp.minimum(rank, 1)
            towards = lax.rem(patch - z + 4, 4)
            held, sent = numer.at[index], weight.at[index]
            sem, wsem = sems.at[index, which], wsems.at[index, which]
            for wanted, keep, give in (
                (0, stays.at[0], swaps.at[0]),
                (1, plus, swap_plus),
                (2, stays.at[1], swaps.at[1]),
                (3, minus, swap_minus),
            ):
                for own_core in range(2):

                    @pl.when((towards == wanted) & (core == own_core))
                    def _():
                        act(pltpu.make_async_copy(held, (give if own_core else keep).at[rank], sem))
                        act(pltpu.make_async_copy(sent, (keep if own_core else give).at[rank], wsem))

    each(tile, lambda copy: copy.start())

    @pl.when(tile == 3)
    def _():
        for index in range(4):
            each(index, lambda copy: copy.wait())


def match_tiles(patches, corners, taps, coeffs, images, variances):
    pair = jax.ShapeDtypeStruct((2, TILE + 16, TILE), BF16)
    quad = jax.ShapeDtypeStruct((2, 2, TILE + 16, TILE), BF16)
    return pl.pallas_call(
        match_kernel,
        grid=(4,),
        in_specs=[pl.BlockSpec(memory_space=pltpu.HBM)] * 6,
        out_specs=[pl.BlockSpec(memory_space=pl.ANY)] * 6,
        out_shape=[quad, pair, pair, quad, pair, pair],
        scratch_shapes=[
            pltpu.SMEM((2, 4), jnp.int32),
            pltpu.SMEM((2, 2, 4), jnp.int32),
            pltpu.VMEM((BASES, 2, TAPS), BF16),
            pltpu.VMEM((BASES, 4, 3), BF16),
            pltpu.VMEM((4, TILE, TILE), BF16),
            pltpu.VMEM((4, TILE, TILE), BF16),
            pltpu.VMEM((BASES, TILE, TILE), BF16),
            pltpu.VMEM((BASES, TILE, TILE), BF16),
            pltpu.VMEM((8, 3 * LANES), F32),
            pltpu.VMEM((BASES, 8, LANES), F32),
            pltpu.VMEM((4, TILE + 16, TILE), BF16),
            pltpu.VMEM((4, TILE + 16, TILE), BF16),
            pltpu.SemaphoreType.DMA((4,)),
            pltpu.SemaphoreType.DMA((2, 4)),
            pltpu.SemaphoreType.DMA((4, 2)),
            pltpu.SemaphoreType.DMA((4, 2)),
        ],
        compiler_params=pltpu.CompilerParams(vmem_limit_bytes=60 << 20),
        cost_estimate=pl.CostEstimate(flops=6 << 30, bytes_accessed=12 << 20, transcendentals=0),
    )(patches, corners, taps, coeffs, images, variances)


def start_kernel(*refs):
    stacks, frame = refs[:-1], refs[-1]
    frame[...] = jnp.zeros_like(frame)
    add_tiles(0, stacks, frame)


def finish_kernel(count, *refs):
    stacks, outs, frame = refs[1 : 1 + count], refs[-5:-1], refs[-1]
    add_tiles(0, stacks, frame)
    pack(frame, outs)


def opposite_kernel(*refs):
    stacks, outs, frame = refs[:-5], refs[-5:-1], refs[-1]
    frame[...] = jnp.zeros_like(frame)
    add_tiles(1, stacks, frame)
    pack(frame, outs)


def add_tiles(far, stacks, frame):
    patch = lax.rem(lax.axis_index("patch") + 2 * far, 4).astype(F32)
    inner = lax.broadcasted_iota(jnp.int32, (1, ROWS, LANES), 1)
    lane = lax.broadcasted_iota(jnp.int32, (1, ROWS, LANES), 2)
    groups = TILE // ROWS

    def add(tile):
        named, tops, lefts = (
            tile[TILE : TILE + 16, part * LANES : (part + 1) * LANES].astype(F32)[0:1] for part in range(3)
        )
        top = jnp.sum(jnp.where(named == patch, tops, 0.0)).astype(jnp.int32)
        left = jnp.sum(jnp.where(named == patch, lefts, 0.0)).astype(jnp.int32)
        first = jnp.minimum(lax.div(left, LANES) * LANES, PATCH_PIX - TILE - LANES)
        shift = left - first
        group, lead = lax.div(top, ROWS), lax.rem(top, ROWS)
        before = jnp.zeros((groups, ROWS, LANES), F32)
        for block in range(5):
            turned = jnp.zeros((groups, ROWS, LANES), F32)
            if block < 4:
                part = tile[0:TILE, block * LANES : (block + 1) * LANES].astype(F32)
                turned = pltpu.roll(part, shift, axis=1).reshape(groups, ROWS, LANES)
                turned = pltpu.roll(turned, lead, axis=1)
            moved = jnp.where(lane >= shift, turned, before)
            before = turned
            nothing = jnp.zeros((1, ROWS, LANES), F32)
            lower = jnp.concatenate([moved, nothing], axis=0)
            upper = jnp.concatenate([nothing, moved], axis=0)
            where = (
                pl.ds(group, groups + 1),
                slice(None),
                pl.ds(pl.multiple_of(first + block * LANES, LANES), LANES),
            )
            frame[where] += jnp.where(inner >= lead, lower, upper)

    for stack in stacks:

        def both(slot, carry, stack=stack):
            add(stack.at[far, slot] if len(stack.shape) == 4 else stack.at[slot])
            return carry

        lax.fori_loop(0, 2, both, 0)


def pack(frame, outs):
    y, x, core, _ = position()
    for out in range(4):
        for part in range(4):
            dx, dy = jnp.where(core == 0, out, part), jnp.where(core == 0, part, out)
            for dc in range(2):
                row = 8 * STRIP * lax.rem(y + dy, 4) + 2 * STRIP * lax.rem(x + dx, 4) + STRIP * lax.rem(core + dc, 2)
                strip = frame[pl.ds(lax.div(row, ROWS), STRIP // ROWS)]
                at = (2 * part + dc) * STRIP
                outs[out][at : at + STRIP, :] = strip.reshape(STRIP, PATCH_PIX).astype(BF16)


SLABS = [jax.ShapeDtypeStruct((SLAB, PATCH_PIX), BF16)] * 4
FRAME = (PATCH_PIX // ROWS + 1, ROWS, PATCH_PIX)


def frame_options(tiles):
    cost = pl.CostEstimate(flops=tiles << 29, bytes_accessed=(5 + tiles) << 20, transcendentals=0)
    return dict(compiler_params=pltpu.CompilerParams(vmem_limit_bytes=36 << 20), cost_estimate=cost)


def opposite_frame(stacks):
    return pl.pallas_call(
        opposite_kernel, out_shape=SLABS, scratch_shapes=[pltpu.VMEM(FRAME, F32)], **frame_options(4)
    )(*stacks)


def start_frame(stacks):
    return pl.pallas_call(start_kernel, out_shape=jax.ShapeDtypeStruct(FRAME, F32), **frame_options(8))(*stacks)


def finish_frame(frame, stacks, after):
    spaces = [pltpu.VMEM] * (1 + len(stacks)) + [pl.ANY]
    return pl.pallas_call(
        functools.partial(finish_kernel, len(stacks)),
        in_specs=[pl.BlockSpec(memory_space=space) for space in spaces],
        out_shape=SLABS + [jax.ShapeDtypeStruct(FRAME, F32)],
        input_output_aliases={0: 4},
        **frame_options(4),
    )(frame, *stacks, after)[:4]


def sum_kernel(count, *refs):
    for part in range(4):
        rows = slice(part * 2 * STRIP, (part + 1) * 2 * STRIP)
        total = refs[0][rows].astype(F32)
        for ref in refs[1:count]:
            total += ref[rows].astype(F32)
        refs[count + part][...] = total.astype(BF16)


def sum_slabs(slabs):
    count = len(slabs)
    out = jax.ShapeDtypeStruct((2 * STRIP, PATCH_PIX), BF16)
    return pl.pallas_call(
        functools.partial(sum_kernel, count),
        out_shape=[out] * 4,
        compiler_params=pltpu.CompilerParams(vmem_limit_bytes=40 << 20),
        cost_estimate=pl.CostEstimate(flops=3 << 20, bytes_accessed=(count + 1) << 20, transcendentals=0),
    )(*slabs)


def spread(pieces, second):
    return [pieces[0]] + [turn(pieces[step], step, second) for step in (1, 3, 2)]


def add_up(pieces):
    return sum(piece.astype(F32) for piece in pieces)


def body(images, variances, kernels, coefficients, intersections, offsets):
    core = lax.rem(lax.axis_index("visit"), 2)
    stays, plus, minus, swaps, swap_plus, swap_minus = match_tiles(
        jnp.transpose(intersections[0]),
        jnp.transpose(offsets[0], (1, 2, 0)),
        jnp.transpose(kernels[0], (1, 0, 2)),
        jnp.transpose(coefficients[0], (1, 0, 2)),
        images[0],
        variances[0],
    )
    swapped = across_core(swaps)
    below, above = across_z(plus, 1), across_z(minus, 3)
    opposite = opposite_frame([stays, swapped])
    summed = add_up(spread(opposite, False)).astype(BF16)
    passed = across_z(summed, 2)
    below_too = across_both(lax.optimization_barrier((swap_plus, below, opposite[0]))[0], 1)
    above_too = across_both(lax.optimization_barrier((swap_minus, above, opposite[0]))[0], 3)
    begun = start_frame([stays, swapped, below, above])
    own = finish_frame(begun, [below_too, above_too], summed)
    pieces = sum_slabs(spread(own, False) + [passed])
    rows = add_up(spread(pieces, True))
    keep, got = rows[:STRIP], across_core(rows[STRIP:])
    numer = jnp.where(core == 0, keep, got)
    weight = jnp.where(core == 0, got, keep)
    return (numer / (weight + 1.0))[None], weight[None]


def solution(mesh):
    return jax.shard_map(
        body,
        mesh=mesh,
        in_specs=(
            P("visit", "patch", None, None),
            P("visit", "patch", None, None),
            P("visit", None, None, None),
            P("visit", "patch", None, None),
            P("visit", "patch", None),
            P("visit", "patch", None, None),
        ),
        out_specs=(P("patch", "visit", None), P("patch", "visit", None)),
        check_vma=False,
    )
```

```python
import functools

import jax
import jax.numpy as jnp
from jax import lax
from jax.experimental import pallas as pl
from jax.experimental.pallas import tpu as pltpu
from jax.sharding import PartitionSpec as P

TAPS = 31
BASES = 3
TILE = 512
PATCH_PIX = 1536
STRIP = 48
LANES = 128
ROWS = 8
SLAB = 384
BF16 = jnp.bfloat16
F32 = jnp.float32


def visit_of(y, x, c):
    return (y * 4 + x) * 2 + c


def chips():
    return [(y, x) for y in range(4) for x in range(4)]


def turn(value, step, second):
    pairs = []
    for y, x in chips():
        for c in range(2):
            along_y = (c == 1) != second
            target = visit_of((y + step) % 4, x, c) if along_y else visit_of(y, (x + step) % 4, c)
            pairs.append((visit_of(y, x, c), target))
    return lax.ppermute(value, "visit", pairs)


def across_z(value, step):
    return lax.ppermute(value, "patch", [(z, (z + step) % 4) for z in range(4)])


def across_core(value):
    pairs = [(visit_of(y, x, c), visit_of(y, x, 1 - c)) for y, x in chips() for c in range(2)]
    return lax.ppermute(value, "visit", pairs)


def across_both(value, step):
    pairs = [
        (visit_of(y, x, c) * 4 + z, visit_of(y, x, 1 - c) * 4 + (z + step) % 4)
        for y, x in chips()
        for c in range(2)
        for z in range(4)
    ]
    return lax.ppermute(value, ("visit", "patch"), pairs)


def position():
    visit = lax.axis_index("visit")
    return lax.div(visit, 8), lax.rem(lax.div(visit, 2), 4), lax.rem(visit, 2), lax.axis_index("patch")


def lane_values(shape, pairs, default):
    lane = lax.broadcasted_iota(jnp.int32, shape, len(shape) - 1)
    out = jnp.full(shape, default, F32)
    for where, value in pairs:
        out = jnp.where(lane == where, value, out)
    return out


def match_kernel(
    patches_in, corners_in, taps_in, coeffs_in, images_in, variances_in, stays, plus, minus, swaps, swap_plus, swap_minus,
    patches, corners, taps, coeffs, images, variances, across, down, lanes, factors, numer, weight,
    in_sems, tile_sems, sems, wsems,
):
    tile = pl.program_id(0)
    loads = [
        [
            pltpu.make_async_copy(images_in.at[index], images.at[index], tile_sems.at[0, index]),
            pltpu.make_async_copy(variances_in.at[index], variances.at[index], tile_sems.at[1, index]),
        ]
        for index in (0, 1, 2, 3, tile)
    ]
    _, _, core, z = position()

    @pl.when(tile == 0)
    def _():
        small = [(patches_in, patches), (corners_in, corners), (taps_in, taps), (coeffs_in, coeffs)]
        copies = [pltpu.make_async_copy(a, b, in_sems.at[k]) for k, (a, b) in enumerate(small)]
        for copy in copies:
            copy.start()
        for pair in loads[:4]:
            for copy in pair:
                copy.start()
        for copy in copies:
            copy.wait()
        lanes[...] = jnp.zeros_like(lanes)
        for basis in range(BASES):
            factors[basis, 0:4, 0:3] = coeffs[basis].astype(F32)
            for axis in range(2):
                lanes[2 * basis + axis : 2 * basis + axis + 1, 0:TAPS] = taps[basis, axis : axis + 1, :].astype(F32)
        for basis in range(BASES):
            for axis in range(2):
                row = jnp.broadcast_to(lanes[2 * basis + axis : 2 * basis + axis + 1, :], (LANES, 3 * LANES))
                band = pltpu.roll(row, LANES - TAPS // 2, axis=1, stride=1, stride_axis=0)
                if axis == 1:
                    band = band.T
                band = band.astype(BF16)
                table = across if axis == 1 else down
                table[basis] = jnp.zeros((TILE, TILE), BF16)
                for block in range(TILE // LANES):
                    first = (block - 1) * LANES
                    low, high = max(first, 0), min(first + 3 * LANES, TILE)
                    span = slice(block * LANES, (block + 1) * LANES)
                    if axis == 1:
                        table[basis, low:high, span] = band[low - first : high - first, :]
                    else:
                        table[basis, span, low:high] = band[:, low - first : high - first]

    rows = lax.broadcasted_iota(jnp.int32, (TILE, 1), 0).astype(F32)
    columns = lax.broadcasted_iota(jnp.int32, (1, TILE), 1).astype(F32)
    rows = (rows - (TILE - 1) / 2.0) / (TILE / 2.0)
    columns = (columns - (TILE - 1) / 2.0) / (TILE / 2.0)
    for copy in loads[4]:
        copy.wait()
    total = jnp.zeros((TILE, TILE), F32)
    for basis in range(BASES):
        middle = jnp.dot(images[tile], across[basis], preferred_element_type=F32).astype(BF16)
        smoothed = jnp.dot(down[basis], middle, preferred_element_type=F32)
        c0, c1, c2 = (factors[basis, pl.ds(tile, 1), k : k + 1] for k in range(3))
        total += ((c0 + c1 * columns) + c2 * rows) * smoothed
    inverse = 1.0 / variances[tile].astype(F32)
    numer[tile, 0:TILE] = (inverse * total).astype(BF16)
    weight[tile, 0:TILE] = inverse.astype(BF16)
    named, tops, lefts = [], [], []
    for which in range(2):
        patch = patches[which, tile].astype(F32)
        named += [(8 * which, patch), (8 * which + 1, patch)]
        for axis, parts in enumerate((tops, lefts)):
            corner = corners[which, axis, tile]
            fine = lax.rem(corner, 32)
            parts += [(8 * which, (corner - fine).astype(F32)), (8 * which + 1, fine.astype(F32))]
    for held in (numer, weight):
        for part, pairs in enumerate((named, tops, lefts)):
            note = lane_values((16, LANES), pairs, -1.0 if part == 0 else 0.0)
            held[tile, TILE : TILE + 16, part * LANES : (part + 1) * LANES] = note.astype(BF16)

    def each(index, act):
        for which in range(2):
            patch = patches[which, index]
            rank = jnp.int32(0)
            for other in range(8):
                before = (2 * index + which > other) & (patches[other % 2, other // 2] == patch)
                rank += jnp.where(before, 1, 0)
            rank = jnp.minimum(rank, 1)
            towards = lax.rem(patch - z + 4, 4)
            held, sent = numer.at[index], weight.at[index]
            sem, wsem = sems.at[index, which], wsems.at[index, which]
            for wanted, keep, give in (
                (0, stays.at[0], swaps.at[0]),
                (1, plus, swap_plus),
                (2, stays.at[1], swaps.at[1]),
                (3, minus, swap_minus),
            ):
                for own_core in range(2):

                    @pl.when((towards == wanted) & (core == own_core))
                    def _():
                        act(pltpu.make_async_copy(held, (give if own_core else keep).at[rank], sem))
                        act(pltpu.make_async_copy(sent, (keep if own_core else give).at[rank], wsem))

    each(tile, lambda copy: copy.start())

    @pl.when(tile == 3)
    def _():
        for index in range(4):
            each(index, lambda copy: copy.wait())


def match_tiles(patches, corners, taps, coeffs, images, variances):
    pair = jax.ShapeDtypeStruct((2, TILE + 16, TILE), BF16)
    quad = jax.ShapeDtypeStruct((2, 2, TILE + 16, TILE), BF16)
    return pl.pallas_call(
        match_kernel,
        grid=(4,),
        in_specs=[pl.BlockSpec(memory_space=pltpu.HBM)] * 6,
        out_specs=[pl.BlockSpec(memory_space=pl.ANY)] * 6,
        out_shape=[quad, pair, pair, quad, pair, pair],
        scratch_shapes=[
            pltpu.SMEM((2, 4), jnp.int32),
            pltpu.SMEM((2, 2, 4), jnp.int32),
            pltpu.VMEM((BASES, 2, TAPS), BF16),
            pltpu.VMEM((BASES, 4, 3), BF16),
            pltpu.VMEM((4, TILE, TILE), BF16),
            pltpu.VMEM((4, TILE, TILE), BF16),
            pltpu.VMEM((BASES, TILE, TILE), BF16),
            pltpu.VMEM((BASES, TILE, TILE), BF16),
            pltpu.VMEM((8, 3 * LANES), F32),
            pltpu.VMEM((BASES, 8, LANES), F32),
            pltpu.VMEM((4, TILE + 16, TILE), BF16),
            pltpu.VMEM((4, TILE + 16, TILE), BF16),
            pltpu.SemaphoreType.DMA((4,)),
            pltpu.SemaphoreType.DMA((2, 4)),
            pltpu.SemaphoreType.DMA((4, 2)),
            pltpu.SemaphoreType.DMA((4, 2)),
        ],
        compiler_params=pltpu.CompilerParams(vmem_limit_bytes=60 << 20),
        cost_estimate=pl.CostEstimate(flops=6 << 30, bytes_accessed=12 << 20, transcendentals=0),
    )(patches, corners, taps, coeffs, images, variances)


def start_kernel(*refs):
    stacks, frame = refs[:-1], refs[-1]
    frame[...] = jnp.zeros_like(frame)
    add_tiles(0, stacks, frame)


def finish_kernel(count, *refs):
    stacks, outs, frame = refs[1 : 1 + count], refs[-5:-1], refs[-1]
    add_tiles(0, stacks, frame)
    pack(frame, outs)


def opposite_kernel(*refs):
    stacks, outs, frame = refs[:-5], refs[-5:-1], refs[-1]
    frame[...] = jnp.zeros_like(frame)
    add_tiles(1, stacks, frame)
    pack(frame, outs)


def add_tiles(far, stacks, frame):
    patch = lax.rem(lax.axis_index("patch") + 2 * far, 4).astype(F32)
    inner = lax.broadcasted_iota(jnp.int32, (1, ROWS, LANES), 1)
    lane = lax.broadcasted_iota(jnp.int32, (1, ROWS, LANES), 2)
    groups = TILE // ROWS

    def add(tile):
        named, tops, lefts = (
            tile[TILE : TILE + 16, part * LANES : (part + 1) * LANES].astype(F32)[0:1] for part in range(3)
        )
        top = jnp.sum(jnp.where(named == patch, tops, 0.0)).astype(jnp.int32)
        left = jnp.sum(jnp.where(named == patch, lefts, 0.0)).astype(jnp.int32)
        first = jnp.minimum(lax.div(left, LANES) * LANES, PATCH_PIX - TILE - LANES)
        shift = left - first
        group, lead = lax.div(top, ROWS), lax.rem(top, ROWS)
        before = jnp.zeros((groups, ROWS, LANES), F32)
        for block in range(5):
            turned = jnp.zeros((groups, ROWS, LANES), F32)
            if block < 4:
                part = tile[0:TILE, block * LANES : (block + 1) * LANES].astype(F32)
                turned = pltpu.roll(part, shift, axis=1).reshape(groups, ROWS, LANES)
                turned = pltpu.roll(turned, lead, axis=1)
            moved = jnp.where(lane >= shift, turned, before)
            before = turned
            nothing = jnp.zeros((1, ROWS, LANES), F32)
            lower = jnp.concatenate([moved, nothing], axis=0)
            upper = jnp.concatenate([nothing, moved], axis=0)
            where = (
                pl.ds(group, groups + 1),
                slice(None),
                pl.ds(pl.multiple_of(first + block * LANES, LANES), LANES),
            )
            frame[where] += jnp.where(inner >= lead, lower, upper)

    for stack in stacks:

        def both(slot, carry, stack=stack):
            add(stack.at[far, slot] if len(stack.shape) == 4 else stack.at[slot])
            return carry

        lax.fori_loop(0, 2, both, 0)


def pack(frame, outs):
    y, x, core, _ = position()
    for out in range(4):
        for part in range(4):
            dx, dy = jnp.where(core == 0, out, part), jnp.where(core == 0, part, out)
            for dc in range(2):
                row = 8 * STRIP * lax.rem(y + dy, 4) + 2 * STRIP * lax.rem(x + dx, 4) + STRIP * lax.rem(core + dc, 2)
                strip = frame[pl.ds(lax.div(row, ROWS), STRIP // ROWS)]
                at = (2 * part + dc) * STRIP
                outs[out][at : at + STRIP, :] = strip.reshape(STRIP, PATCH_PIX).astype(BF16)


SLABS = [jax.ShapeDtypeStruct((SLAB, PATCH_PIX), BF16)] * 4
FRAME = (PATCH_PIX // ROWS + 1, ROWS, PATCH_PIX)


def frame_options(tiles):
    cost = pl.CostEstimate(flops=tiles << 29, bytes_accessed=(5 + tiles) << 20, transcendentals=0)
    return dict(compiler_params=pltpu.CompilerParams(vmem_limit_bytes=36 << 20), cost_estimate=cost)


def opposite_frame(stacks):
    return pl.pallas_call(
        opposite_kernel, out_shape=SLABS, scratch_shapes=[pltpu.VMEM(FRAME, F32)], **frame_options(4)
    )(*stacks)


def start_frame(stacks):
    return pl.pallas_call(start_kernel, out_shape=jax.ShapeDtypeStruct(FRAME, F32), **frame_options(8))(*stacks)


def finish_frame(frame, stacks, after):
    spaces = [pltpu.VMEM] * (1 + len(stacks)) + [pl.ANY]
    return pl.pallas_call(
        functools.partial(finish_kernel, len(stacks)),
        in_specs=[pl.BlockSpec(memory_space=space) for space in spaces],
        out_shape=SLABS + [jax.ShapeDtypeStruct(FRAME, F32)],
        input_output_aliases={0: 4},
        **frame_options(4),
    )(frame, *stacks, after)[:4]


def sum_kernel(count, *refs):
    for part in range(4):
        rows = slice(part * 2 * STRIP, (part + 1) * 2 * STRIP)
        total = refs[0][rows].astype(F32)
        for ref in refs[1:count]:
            total += ref[rows].astype(F32)
        refs[count + part][...] = total.astype(BF16)


def sum_slabs(slabs):
    count = len(slabs)
    out = jax.ShapeDtypeStruct((2 * STRIP, PATCH_PIX), BF16)
    return pl.pallas_call(
        functools.partial(sum_kernel, count),
        out_shape=[out] * 4,
        compiler_params=pltpu.CompilerParams(vmem_limit_bytes=40 << 20),
        cost_estimate=pl.CostEstimate(flops=3 << 20, bytes_accessed=(count + 1) << 20, transcendentals=0),
    )(*slabs)


def spread(pieces, second):
    return [pieces[0]] + [turn(pieces[step], step, second) for step in (1, 3, 2)]


def add_up(pieces):
    return sum(piece.astype(F32) for piece in pieces)


def body(images, variances, kernels, coefficients, intersections, offsets):
    core = lax.rem(lax.axis_index("visit"), 2)
    stays, plus, minus, swaps, swap_plus, swap_minus = match_tiles(
        jnp.transpose(intersections[0]),
        jnp.transpose(offsets[0], (1, 2, 0)),
        jnp.transpose(kernels[0], (1, 0, 2)),
        jnp.transpose(coefficients[0], (1, 0, 2)),
        images[0],
        variances[0],
    )
    swapped = across_core(swaps)
    below, above = across_z(plus, 1), across_z(minus, 3)
    opposite = opposite_frame([stays, swapped])
    summed = add_up(spread(sum_slabs(spread(opposite, False)), True)).astype(BF16)
    passed = across_z(summed, 2)
    below_too = across_both(lax.optimization_barrier((swap_plus, below, opposite[0]))[0], 1)
    above_too = across_both(lax.optimization_barrier((swap_minus, above, opposite[0]))[0], 3)
    begun = start_frame([stays, swapped, below, above])
    own = finish_frame(begun, [below_too, above_too], summed)
    pieces = sum_slabs(spread(own, False))
    rows = add_up(spread(pieces, True) + [passed])
    keep, got = rows[:STRIP], across_core(rows[STRIP:])
    numer = jnp.where(core == 0, keep, got)
    weight = jnp.where(core == 0, got, keep)
    return (numer / (weight + 1.0))[None], weight[None]


def solution(mesh):
    return jax.shard_map(
        body,
        mesh=mesh,
        in_specs=(
            P("visit", "patch", None, None),
            P("visit", "patch", None, None),
            P("visit", None, None, None),
            P("visit", "patch", None, None),
            P("visit", "patch", None),
            P("visit", "patch", None, None),
        ),
        out_specs=(P("patch", "visit", None), P("patch", "visit", None)),
        check_vma=False,
    )
```

```python
import functools

import jax
import jax.numpy as jnp
from jax import lax
from jax.experimental import pallas as pl
from jax.experimental.pallas import tpu as pltpu
from jax.sharding import PartitionSpec as P

TAPS = 31
BASES = 3
TILE = 512
PATCH_PIX = 1536
STRIP = 48
LANES = 128
ROWS = 8
SLAB = 384
WINDOWS = ((0, 0), (1, 64), (1, 192), (2, 256))
BF16 = jnp.bfloat16
F32 = jnp.float32


def visit_of(y, x, c):
    return (y * 4 + x) * 2 + c


def chips():
    return [(y, x) for y in range(4) for x in range(4)]


def turn(value, step, second):
    pairs = []
    for y, x in chips():
        for c in range(2):
            along_y = (c == 1) != second
            target = visit_of((y + step) % 4, x, c) if along_y else visit_of(y, (x + step) % 4, c)
            pairs.append((visit_of(y, x, c), target))
    return lax.ppermute(value, "visit", pairs)


def across_z(value, step):
    return lax.ppermute(value, "patch", [(z, (z + step) % 4) for z in range(4)])


def across_core(value):
    pairs = [(visit_of(y, x, c), visit_of(y, x, 1 - c)) for y, x in chips() for c in range(2)]
    return lax.ppermute(value, "visit", pairs)


def across_both(value, step):
    pairs = [
        (visit_of(y, x, c) * 4 + z, visit_of(y, x, 1 - c) * 4 + (z + step) % 4)
        for y, x in chips()
        for c in range(2)
        for z in range(4)
    ]
    return lax.ppermute(value, ("visit", "patch"), pairs)


def position():
    visit = lax.axis_index("visit")
    return lax.div(visit, 8), lax.rem(lax.div(visit, 2), 4), lax.rem(visit, 2), lax.axis_index("patch")


def lane_values(shape, pairs, default):
    lane = lax.broadcasted_iota(jnp.int32, shape, len(shape) - 1)
    out = jnp.full(shape, default, F32)
    for where, value in pairs:
        out = jnp.where(lane == where, value, out)
    return out


def match_kernel(
    patches_in, corners_in, taps_in, coeffs_in, images_in, variances_in, stays, plus, minus, swaps, swap_plus, swap_minus,
    patches, corners, taps, coeffs, images, variances, across, down, lanes, factors, numer, weight,
    in_sems, tile_sems, sems, wsems,
):
    tile = pl.program_id(0)
    loads = [
        [
            pltpu.make_async_copy(images_in.at[index], images.at[index], tile_sems.at[0, index]),
            pltpu.make_async_copy(variances_in.at[index], variances.at[index], tile_sems.at[1, index]),
        ]
        for index in (0, 1, 2, 3, tile)
    ]
    _, _, core, z = position()

    @pl.when(tile == 0)
    def _():
        small = [(patches_in, patches), (corners_in, corners), (taps_in, taps), (coeffs_in, coeffs)]
        copies = [pltpu.make_async_copy(a, b, in_sems.at[k]) for k, (a, b) in enumerate(small)]
        for copy in copies:
            copy.start()
        for pair in loads[:4]:
            for copy in pair:
                copy.start()
        for copy in copies:
            copy.wait()
        lanes[...] = jnp.zeros_like(lanes)
        for basis in range(BASES):
            factors[basis, 0:4, 0:3] = coeffs[basis].astype(F32)
            for axis in range(2):
                lanes[2 * basis + axis : 2 * basis + axis + 1, 0:TAPS] = taps[basis, axis : axis + 1, :].astype(F32)
        for basis in range(BASES):
            for axis in range(2):
                row = jnp.broadcast_to(lanes[2 * basis + axis : 2 * basis + axis + 1, :], (LANES, 3 * LANES))
                band = pltpu.roll(row, LANES - TAPS // 2, axis=1, stride=1, stride_axis=0)
                if axis == 0:
                    centred = pltpu.roll(row, LANES // 2 - TAPS // 2, axis=1, stride=1, stride_axis=0)
                    down[basis, 0] = band[:, LANES:].astype(BF16)
                    down[basis, 1] = centred[:, : 2 * LANES].astype(BF16)
                    down[basis, 2] = band[:, : 2 * LANES].astype(BF16)
                    continue
                band = band.T.astype(BF16)
                across[basis] = jnp.zeros((TILE, TILE), BF16)
                for block in range(TILE // LANES):
                    first = (block - 1) * LANES
                    low, high = max(first, 0), min(first + 3 * LANES, TILE)
                    span = slice(block * LANES, (block + 1) * LANES)
                    across[basis, low:high, span] = band[low - first : high - first, :]

    rows = lax.broadcasted_iota(jnp.int32, (TILE, 1), 0).astype(F32)
    columns = lax.broadcasted_iota(jnp.int32, (1, TILE), 1).astype(F32)
    rows = (rows - (TILE - 1) / 2.0) / (TILE / 2.0)
    columns = (columns - (TILE - 1) / 2.0) / (TILE / 2.0)
    for copy in loads[4]:
        copy.wait()
    total = jnp.zeros((TILE, TILE), F32)
    for basis in range(BASES):
        middle = jnp.dot(images[tile], across[basis], preferred_element_type=F32).astype(BF16)
        smoothed = jnp.concatenate(
            [
                jnp.dot(down[basis, kind], middle[first : first + 2 * LANES], preferred_element_type=F32)
                for kind, first in WINDOWS
            ],
            axis=0,
        )
        c0, c1, c2 = (factors[basis, pl.ds(tile, 1), k : k + 1] for k in range(3))
        total += ((c0 + c1 * columns) + c2 * rows) * smoothed
    inverse = 1.0 / variances[tile].astype(F32)
    numer[tile, 0:TILE] = (inverse * total).astype(BF16)
    weight[tile, 0:TILE] = inverse.astype(BF16)
    named, tops, lefts = [], [], []
    for which in range(2):
        patch = patches[which, tile].astype(F32)
        named += [(8 * which, patch), (8 * which + 1, patch)]
        for axis, parts in enumerate((tops, lefts)):
            corner = corners[which, axis, tile]
            fine = lax.rem(corner, 32)
            parts += [(8 * which, (corner - fine).astype(F32)), (8 * which + 1, fine.astype(F32))]
    for held in (numer, weight):
        for part, pairs in enumerate((named, tops, lefts)):
            note = lane_values((16, LANES), pairs, -1.0 if part == 0 else 0.0)
            held[tile, TILE : TILE + 16, part * LANES : (part + 1) * LANES] = note.astype(BF16)

    def each(index, act):
        for which in range(2):
            patch = patches[which, index]
            rank = jnp.int32(0)
            for other in range(8):
                before = (2 * index + which > other) & (patches[other % 2, other // 2] == patch)
                rank += jnp.where(before, 1, 0)
            rank = jnp.minimum(rank, 1)
            towards = lax.rem(patch - z + 4, 4)
            held, sent = numer.at[index], weight.at[index]
            sem, wsem = sems.at[index, which], wsems.at[index, which]
            for wanted, keep, give in (
                (0, stays.at[0], swaps.at[0]),
                (1, plus, swap_plus),
                (2, stays.at[1], swaps.at[1]),
                (3, minus, swap_minus),
            ):
                for own_core in range(2):

                    @pl.when((towards == wanted) & (core == own_core))
                    def _():
                        act(pltpu.make_async_copy(held, (give if own_core else keep).at[rank], sem))
                        act(pltpu.make_async_copy(sent, (keep if own_core else give).at[rank], wsem))

    each(tile, lambda copy: copy.start())

    @pl.when(tile == 3)
    def _():
        for index in range(4):
            each(index, lambda copy: copy.wait())


def match_tiles(patches, corners, taps, coeffs, images, variances):
    pair = jax.ShapeDtypeStruct((2, TILE + 16, TILE), BF16)
    quad = jax.ShapeDtypeStruct((2, 2, TILE + 16, TILE), BF16)
    return pl.pallas_call(
        match_kernel,
        grid=(4,),
        in_specs=[pl.BlockSpec(memory_space=pltpu.HBM)] * 6,
        out_specs=[pl.BlockSpec(memory_space=pl.ANY)] * 6,
        out_shape=[quad, pair, pair, quad, pair, pair],
        scratch_shapes=[
            pltpu.SMEM((2, 4), jnp.int32),
            pltpu.SMEM((2, 2, 4), jnp.int32),
            pltpu.VMEM((BASES, 2, TAPS), BF16),
            pltpu.VMEM((BASES, 4, 3), BF16),
            pltpu.VMEM((4, TILE, TILE), BF16),
            pltpu.VMEM((4, TILE, TILE), BF16),
            pltpu.VMEM((BASES, TILE, TILE), BF16),
            pltpu.VMEM((BASES, 3, LANES, 2 * LANES), BF16),
            pltpu.VMEM((8, 3 * LANES), F32),
            pltpu.VMEM((BASES, 8, LANES), F32),
            pltpu.VMEM((4, TILE + 16, TILE), BF16),
            pltpu.VMEM((4, TILE + 16, TILE), BF16),
            pltpu.SemaphoreType.DMA((4,)),
            pltpu.SemaphoreType.DMA((2, 4)),
            pltpu.SemaphoreType.DMA((4, 2)),
            pltpu.SemaphoreType.DMA((4, 2)),
        ],
        compiler_params=pltpu.CompilerParams(vmem_limit_bytes=60 << 20),
        cost_estimate=pl.CostEstimate(flops=6 << 30, bytes_accessed=12 << 20, transcendentals=0),
    )(patches, corners, taps, coeffs, images, variances)


def start_kernel(*refs):
    stacks, frame = refs[:-1], refs[-1]
    frame[...] = jnp.zeros_like(frame)
    add_tiles(0, stacks, frame)


def finish_kernel(count, *refs):
    stacks, outs, frame = refs[1 : 1 + count], refs[-5:-1], refs[-1]
    add_tiles(0, stacks, frame)
    pack(frame, outs)


def opposite_kernel(*refs):
    stacks, outs, frame = refs[:-5], refs[-5:-1], refs[-1]
    frame[...] = jnp.zeros_like(frame)
    add_tiles(1, stacks, frame)
    pack(frame, outs)


def add_tiles(far, stacks, frame):
    patch = lax.rem(lax.axis_index("patch") + 2 * far, 4).astype(F32)
    inner = lax.broadcasted_iota(jnp.int32, (1, ROWS, LANES), 1)
    lane = lax.broadcasted_iota(jnp.int32, (1, ROWS, LANES), 2)
    groups = TILE // ROWS

    def add(tile):
        named, tops, lefts = (
            tile[TILE : TILE + 16, part * LANES : (part + 1) * LANES].astype(F32)[0:1] for part in range(3)
        )
        top = jnp.sum(jnp.where(named == patch, tops, 0.0)).astype(jnp.int32)
        left = jnp.sum(jnp.where(named == patch, lefts, 0.0)).astype(jnp.int32)
        first = jnp.minimum(lax.div(left, LANES) * LANES, PATCH_PIX - TILE - LANES)
        shift = left - first
        group, lead = lax.div(top, ROWS), lax.rem(top, ROWS)
        before = jnp.zeros((groups, ROWS, LANES), F32)
        for block in range(5):
            turned = jnp.zeros((groups, ROWS, LANES), F32)
            if block < 4:
                part = tile[0:TILE, block * LANES : (block + 1) * LANES].astype(F32)
                turned = pltpu.roll(part, shift, axis=1).reshape(groups, ROWS, LANES)
                turned = pltpu.roll(turned, lead, axis=1)
            moved = jnp.where(lane >= shift, turned, before)
            before = turned
            nothing = jnp.zeros((1, ROWS, LANES), F32)
            lower = jnp.concatenate([moved, nothing], axis=0)
            upper = jnp.concatenate([nothing, moved], axis=0)
            where = (
                pl.ds(group, groups + 1),
                slice(None),
                pl.ds(pl.multiple_of(first + block * LANES, LANES), LANES),
            )
            frame[where] += jnp.where(inner >= lead, lower, upper)

    for stack in stacks:

        def both(slot, carry, stack=stack):
            add(stack.at[far, slot] if len(stack.shape) == 4 else stack.at[slot])
            return carry

        lax.fori_loop(0, 2, both, 0)


def pack(frame, outs):
    y, x, core, _ = position()
    for out in range(4):
        for part in range(4):
            dx, dy = jnp.where(core == 0, out, part), jnp.where(core == 0, part, out)
            for dc in range(2):
                row = 8 * STRIP * lax.rem(y + dy, 4) + 2 * STRIP * lax.rem(x + dx, 4) + STRIP * lax.rem(core + dc, 2)
                strip = frame[pl.ds(lax.div(row, ROWS), STRIP // ROWS)]
                at = (2 * part + dc) * STRIP
                outs[out][at : at + STRIP, :] = strip.reshape(STRIP, PATCH_PIX).astype(BF16)


SLABS = [jax.ShapeDtypeStruct((SLAB, PATCH_PIX), BF16)] * 4
FRAME = (PATCH_PIX // ROWS + 1, ROWS, PATCH_PIX)


def frame_options(tiles, grant):
    cost = pl.CostEstimate(flops=tiles << 29, bytes_accessed=(5 + tiles) << 20, transcendentals=0)
    return dict(compiler_params=pltpu.CompilerParams(vmem_limit_bytes=grant << 20), cost_estimate=cost)


def opposite_frame(stacks):
    return pl.pallas_call(
        opposite_kernel, out_shape=SLABS, scratch_shapes=[pltpu.VMEM(FRAME, F32)], **frame_options(4, 22)
    )(*stacks)


def start_frame(stacks):
    return pl.pallas_call(start_kernel, out_shape=jax.ShapeDtypeStruct(FRAME, F32), **frame_options(8, 20))(*stacks)


def finish_frame(frame, stacks, after):
    spaces = [pltpu.VMEM] * (1 + len(stacks)) + [pl.ANY]
    return pl.pallas_call(
        functools.partial(finish_kernel, len(stacks)),
        in_specs=[pl.BlockSpec(memory_space=space) for space in spaces],
        out_shape=SLABS + [jax.ShapeDtypeStruct(FRAME, F32)],
        input_output_aliases={0: 4},
        **frame_options(4, 30),
    )(frame, *stacks, after)[:4]


def sum_kernel(count, *refs):
    for part in range(4):
        rows = slice(part * 2 * STRIP, (part + 1) * 2 * STRIP)
        total = refs[0][rows].astype(F32)
        for ref in refs[1:count]:
            total += ref[rows].astype(F32)
        refs[count + part][...] = total.astype(BF16)


def sum_slabs(slabs):
    count = len(slabs)
    out = jax.ShapeDtypeStruct((2 * STRIP, PATCH_PIX), BF16)
    return pl.pallas_call(
        functools.partial(sum_kernel, count),
        out_shape=[out] * 4,
        compiler_params=pltpu.CompilerParams(vmem_limit_bytes=12 << 20),
        cost_estimate=pl.CostEstimate(flops=3 << 20, bytes_accessed=(count + 1) << 20, transcendentals=0),
    )(*slabs)


def spread(pieces, second):
    return [pieces[0]] + [turn(pieces[step], step, second) for step in (1, 3, 2)]


def add_up(pieces):
    return sum(piece.astype(F32) for piece in pieces)


def body(images, variances, kernels, coefficients, intersections, offsets):
    core = lax.rem(lax.axis_index("visit"), 2)
    stays, plus, minus, swaps, swap_plus, swap_minus = match_tiles(
        jnp.transpose(intersections[0]),
        jnp.transpose(offsets[0], (1, 2, 0)),
        jnp.transpose(kernels[0], (1, 0, 2)),
        jnp.transpose(coefficients[0], (1, 0, 2)),
        images[0],
        variances[0],
    )
    swapped = across_core(swaps)
    below, above = across_z(plus, 1), across_z(minus, 3)
    opposite = opposite_frame([stays, swapped])
    summed = add_up(spread(sum_slabs(spread(opposite, False)), True)).astype(BF16)
    passed = across_z(summed, 2)
    below_too = across_both(lax.optimization_barrier((swap_plus, below, opposite[0]))[0], 1)
    above_too = across_both(lax.optimization_barrier((swap_minus, above, opposite[0]))[0], 3)
    begun = start_frame([stays, swapped, below, above])
    own = finish_frame(begun, [below_too, above_too], summed)
    pieces = sum_slabs(spread(own, False))
    rows = add_up(spread(pieces, True) + [passed])
    keep, got = rows[:STRIP], across_core(rows[STRIP:])
    numer = jnp.where(core == 0, keep, got)
    weight = jnp.where(core == 0, got, keep)
    return (numer / (weight + 1.0))[None], weight[None]


def solution(mesh):
    return jax.shard_map(
        body,
        mesh=mesh,
        in_specs=(
            P("visit", "patch", None, None),
            P("visit", "patch", None, None),
            P("visit", None, None, None),
            P("visit", "patch", None, None),
            P("visit", "patch", None),
            P("visit", "patch", None, None),
        ),
        out_specs=(P("patch", "visit", None), P("patch", "visit", None)),
        check_vma=False,
    )
```

```python
import functools

import jax
import jax.numpy as jnp
from jax import lax
from jax.experimental import pallas as pl
from jax.experimental.pallas import tpu as pltpu
from jax.sharding import PartitionSpec as P

TAPS = 31
BASES = 3
TILE = 512
PATCH_PIX = 1536
STRIP = 48
LANES = 128
ROWS = 8
SLAB = 384
WINDOWS = ((0, 0), (1, 64), (1, 192), (2, 256))
BF16 = jnp.bfloat16
F32 = jnp.float32


def visit_of(y, x, c):
    return (y * 4 + x) * 2 + c


def chips():
    return [(y, x) for y in range(4) for x in range(4)]


def turn(value, step, second):
    pairs = []
    for y, x in chips():
        for c in range(2):
            along_y = (c == 1) != second
            target = visit_of((y + step) % 4, x, c) if along_y else visit_of(y, (x + step) % 4, c)
            pairs.append((visit_of(y, x, c), target))
    return lax.ppermute(value, "visit", pairs)


def across_z(value, step):
    return lax.ppermute(value, "patch", [(z, (z + step) % 4) for z in range(4)])


def across_core(value):
    pairs = [(visit_of(y, x, c), visit_of(y, x, 1 - c)) for y, x in chips() for c in range(2)]
    return lax.ppermute(value, "visit", pairs)


def across_both(value, step):
    pairs = [
        (visit_of(y, x, c) * 4 + z, visit_of(y, x, 1 - c) * 4 + (z + step) % 4)
        for y, x in chips()
        for c in range(2)
        for z in range(4)
    ]
    return lax.ppermute(value, ("visit", "patch"), pairs)


def position():
    visit = lax.axis_index("visit")
    return lax.div(visit, 8), lax.rem(lax.div(visit, 2), 4), lax.rem(visit, 2), lax.axis_index("patch")


def lane_values(shape, pairs, default):
    lane = lax.broadcasted_iota(jnp.int32, shape, len(shape) - 1)
    out = jnp.full(shape, default, F32)
    for where, value in pairs:
        out = jnp.where(lane == where, value, out)
    return out


def match_kernel(
    patches_in, corners_in, taps_in, coeffs_in, images_in, variances_in, stays, plus, minus, swaps, swap_plus, swap_minus,
    patches, corners, taps, coeffs, images, variances, across, down, lanes, factors, numer, weight,
    in_sems, tile_sems, sems, wsems,
):
    tile = pl.program_id(0)
    loads = [
        [
            pltpu.make_async_copy(images_in.at[index], images.at[index], tile_sems.at[0, index]),
            pltpu.make_async_copy(variances_in.at[index], variances.at[index], tile_sems.at[1, index]),
        ]
        for index in (0, 1, 2, 3, tile)
    ]
    _, _, core, z = position()

    @pl.when(tile == 0)
    def _():
        small = [(patches_in, patches), (corners_in, corners), (taps_in, taps), (coeffs_in, coeffs)]
        copies = [pltpu.make_async_copy(a, b, in_sems.at[k]) for k, (a, b) in enumerate(small)]
        for copy in copies:
            copy.start()
        for pair in loads[:4]:
            for copy in pair:
                copy.start()
        for copy in copies:
            copy.wait()
        lanes[...] = jnp.zeros_like(lanes)
        for basis in range(BASES):
            factors[basis, 0:4, 0:3] = coeffs[basis].astype(F32)
            for axis in range(2):
                lanes[2 * basis + axis : 2 * basis + axis + 1, 0:TAPS] = taps[basis, axis : axis + 1, :].astype(F32)
        for basis in range(BASES):
            for axis in range(2):
                row = jnp.broadcast_to(lanes[2 * basis + axis : 2 * basis + axis + 1, :], (LANES, 3 * LANES))
                band = pltpu.roll(row, LANES - TAPS // 2, axis=1, stride=1, stride_axis=0)
                if axis == 0:
                    centred = pltpu.roll(row, LANES // 2 - TAPS // 2, axis=1, stride=1, stride_axis=0)
                    down[basis, 0] = band[:, LANES:].astype(BF16)
                    down[basis, 1] = centred[:, : 2 * LANES].astype(BF16)
                    down[basis, 2] = band[:, : 2 * LANES].astype(BF16)
                    continue
                band = band.T.astype(BF16)
                across[basis] = jnp.zeros((TILE, TILE), BF16)
                for block in range(TILE // LANES):
                    first = (block - 1) * LANES
                    low, high = max(first, 0), min(first + 3 * LANES, TILE)
                    span = slice(block * LANES, (block + 1) * LANES)
                    across[basis, low:high, span] = band[low - first : high - first, :]

    rows = lax.broadcasted_iota(jnp.int32, (TILE, 1), 0).astype(F32)
    columns = lax.broadcasted_iota(jnp.int32, (1, TILE), 1).astype(F32)
    rows = (rows - (TILE - 1) / 2.0) / (TILE / 2.0)
    columns = (columns - (TILE - 1) / 2.0) / (TILE / 2.0)
    for copy in loads[4]:
        copy.wait()
    total = jnp.zeros((TILE, TILE), F32)
    for basis in range(BASES):
        middle = jnp.dot(images[tile], across[basis], preferred_element_type=F32).astype(BF16)
        smoothed = jnp.concatenate(
            [
                jnp.dot(down[basis, kind], middle[first : first + 2 * LANES], preferred_element_type=F32)
                for kind, first in WINDOWS
            ],
            axis=0,
        )
        c0, c1, c2 = (factors[basis, pl.ds(tile, 1), k : k + 1] for k in range(3))
        total += ((c0 + c1 * columns) + c2 * rows) * smoothed
    inverse = 1.0 / variances[tile].astype(F32)
    numer[tile, 0:TILE] = (inverse * total).astype(BF16)
    weight[tile, 0:TILE] = inverse.astype(BF16)
    named, tops, lefts = [], [], []
    for which in range(2):
        patch = patches[which, tile].astype(F32)
        named += [(8 * which, patch), (8 * which + 1, patch)]
        for axis, parts in enumerate((tops, lefts)):
            corner = corners[which, axis, tile]
            fine = lax.rem(corner, 32)
            parts += [(8 * which, (corner - fine).astype(F32)), (8 * which + 1, fine.astype(F32))]
    for held in (numer, weight):
        for part, pairs in enumerate((named, tops, lefts)):
            note = lane_values((16, LANES), pairs, -1.0 if part == 0 else 0.0)
            held[tile, TILE : TILE + 16, part * LANES : (part + 1) * LANES] = note.astype(BF16)

    def each(index, act):
        for which in range(2):
            patch = patches[which, index]
            rank = jnp.int32(0)
            for other in range(8):
                before = (2 * index + which > other) & (patches[other % 2, other // 2] == patch)
                rank += jnp.where(before, 1, 0)
            rank = jnp.minimum(rank, 1)
            towards = lax.rem(patch - z + 4, 4)
            held, sent = numer.at[index], weight.at[index]
            sem, wsem = sems.at[index, which], wsems.at[index, which]
            for wanted, keep, give in (
                (0, stays.at[0], swaps.at[0]),
                (1, plus, swap_plus),
                (2, stays.at[1], swaps.at[1]),
                (3, minus, swap_minus),
            ):
                for own_core in range(2):

                    @pl.when((towards == wanted) & (core == own_core))
                    def _():
                        act(pltpu.make_async_copy(held, (give if own_core else keep).at[rank], sem))
                        act(pltpu.make_async_copy(sent, (keep if own_core else give).at[rank], wsem))

    each(tile, lambda copy: copy.start())

    @pl.when(tile == 3)
    def _():
        for index in range(4):
            each(index, lambda copy: copy.wait())


def match_tiles(patches, corners, taps, coeffs, images, variances):
    pair = jax.ShapeDtypeStruct((2, TILE + 16, TILE), BF16)
    quad = jax.ShapeDtypeStruct((2, 2, TILE + 16, TILE), BF16)
    return pl.pallas_call(
        match_kernel,
        grid=(4,),
        in_specs=[pl.BlockSpec(memory_space=pltpu.HBM)] * 6,
        out_specs=[pl.BlockSpec(memory_space=pl.ANY)] * 6,
        out_shape=[quad, pair, pair, quad, pair, pair],
        scratch_shapes=[
            pltpu.SMEM((2, 4), jnp.int32),
            pltpu.SMEM((2, 2, 4), jnp.int32),
            pltpu.VMEM((BASES, 2, TAPS), BF16),
            pltpu.VMEM((BASES, 4, 3), BF16),
            pltpu.VMEM((4, TILE, TILE), BF16),
            pltpu.VMEM((4, TILE, TILE), BF16),
            pltpu.VMEM((BASES, TILE, TILE), BF16),
            pltpu.VMEM((BASES, 3, LANES, 2 * LANES), BF16),
            pltpu.VMEM((8, 3 * LANES), F32),
            pltpu.VMEM((BASES, 8, LANES), F32),
            pltpu.VMEM((4, TILE + 16, TILE), BF16),
            pltpu.VMEM((4, TILE + 16, TILE), BF16),
            pltpu.SemaphoreType.DMA((4,)),
            pltpu.SemaphoreType.DMA((2, 4)),
            pltpu.SemaphoreType.DMA((4, 2)),
            pltpu.SemaphoreType.DMA((4, 2)),
        ],
        compiler_params=pltpu.CompilerParams(vmem_limit_bytes=60 << 20),
        cost_estimate=pl.CostEstimate(flops=6 << 30, bytes_accessed=12 << 20, transcendentals=0),
    )(patches, corners, taps, coeffs, images, variances)


def start_kernel(*refs):
    stacks, frame = refs[:-1], refs[-1]
    frame[...] = jnp.zeros_like(frame)
    add_tiles(0, stacks, frame)


def finish_kernel(count, *refs):
    frame, stacks, outs = refs[0], refs[1 : 1 + count], refs[-5:-1]
    add_tiles(0, stacks, frame)
    pack(frame, outs)


def opposite_kernel(*refs):
    stacks, outs, frame = refs[:-5], refs[-5:-1], refs[-1]
    frame[...] = jnp.zeros_like(frame)
    add_tiles(1, stacks, frame)
    pack(frame, outs)


def add_tiles(far, stacks, frame):
    patch = lax.rem(lax.axis_index("patch") + 2 * far, 4).astype(F32)
    inner = lax.broadcasted_iota(jnp.int32, (1, ROWS, LANES), 1)
    lane = lax.broadcasted_iota(jnp.int32, (1, ROWS, LANES), 2)
    groups = TILE // ROWS

    def add(tile):
        named, tops, lefts = (
            tile[TILE : TILE + 16, part * LANES : (part + 1) * LANES].astype(F32)[0:1] for part in range(3)
        )
        top = jnp.sum(jnp.where(named == patch, tops, 0.0)).astype(jnp.int32)
        left = jnp.sum(jnp.where(named == patch, lefts, 0.0)).astype(jnp.int32)
        first = jnp.minimum(lax.div(left, LANES) * LANES, PATCH_PIX - TILE - LANES)
        shift = left - first
        group, lead = lax.div(top, ROWS), lax.rem(top, ROWS)
        before = jnp.zeros((groups, ROWS, LANES), F32)
        for block in range(5):
            turned = jnp.zeros((groups, ROWS, LANES), F32)
            if block < 4:
                part = tile[0:TILE, block * LANES : (block + 1) * LANES].astype(F32)
                turned = pltpu.roll(part, shift, axis=1).reshape(groups, ROWS, LANES)
                turned = pltpu.roll(turned, lead, axis=1)
            moved = jnp.where(lane >= shift, turned, before)
            before = turned
            nothing = jnp.zeros((1, ROWS, LANES), F32)
            lower = jnp.concatenate([moved, nothing], axis=0)
            upper = jnp.concatenate([nothing, moved], axis=0)
            where = (
                pl.ds(group, groups + 1),
                slice(None),
                pl.ds(pl.multiple_of(first + block * LANES, LANES), LANES),
            )
            frame[where] += jnp.where(inner >= lead, lower, upper)

    for stack in stacks:

        def both(slot, carry, stack=stack):
            add(stack.at[far, slot] if len(stack.shape) == 4 else stack.at[slot])
            return carry

        lax.fori_loop(0, 2, both, 0)


def pack(frame, outs):
    y, x, core, _ = position()
    for out in range(4):
        for part in range(4):
            dx, dy = jnp.where(core == 0, out, part), jnp.where(core == 0, part, out)
            for dc in range(2):
                row = 8 * STRIP * lax.rem(y + dy, 4) + 2 * STRIP * lax.rem(x + dx, 4) + STRIP * lax.rem(core + dc, 2)
                strip = frame[pl.ds(lax.div(row, ROWS), STRIP // ROWS)]
                at = (2 * part + dc) * STRIP
                outs[out][at : at + STRIP, :] = strip.reshape(STRIP, PATCH_PIX).astype(BF16)


SLABS = [jax.ShapeDtypeStruct((SLAB, PATCH_PIX), BF16)] * 4
FRAME = (PATCH_PIX // ROWS + 1, ROWS, PATCH_PIX)


def frame_options(tiles, grant):
    cost = pl.CostEstimate(flops=tiles << 29, bytes_accessed=(5 + tiles) << 20, transcendentals=0)
    return dict(compiler_params=pltpu.CompilerParams(vmem_limit_bytes=grant << 20), cost_estimate=cost)


def opposite_frame(stacks):
    return pl.pallas_call(
        opposite_kernel, out_shape=SLABS, scratch_shapes=[pltpu.VMEM(FRAME, F32)], **frame_options(4, 22)
    )(*stacks)


def start_frame(stacks):
    return pl.pallas_call(start_kernel, out_shape=jax.ShapeDtypeStruct(FRAME, F32), **frame_options(8, 20))(*stacks)


def finish_frame(frame, stacks, after):
    spaces = [pltpu.VMEM] * (1 + len(stacks)) + [pl.ANY]
    return pl.pallas_call(
        functools.partial(finish_kernel, len(stacks)),
        in_specs=[pl.BlockSpec(memory_space=space) for space in spaces],
        out_shape=SLABS + [jax.ShapeDtypeStruct(FRAME, F32)],
        input_output_aliases={0: 4},
        **frame_options(4, 30),
    )(frame, *stacks, after)[:4]


def sum_kernel(count, *refs):
    for part in range(4):
        rows = slice(part * 2 * STRIP, (part + 1) * 2 * STRIP)
        total = refs[0][rows].astype(F32)
        for ref in refs[1:count]:
            total += ref[rows].astype(F32)
        refs[count + part][...] = total.astype(BF16)


def sum_slabs(slabs):
    count = len(slabs)
    out = jax.ShapeDtypeStruct((2 * STRIP, PATCH_PIX), BF16)
    return pl.pallas_call(
        functools.partial(sum_kernel, count),
        out_shape=[out] * 4,
        compiler_params=pltpu.CompilerParams(vmem_limit_bytes=12 << 20),
        cost_estimate=pl.CostEstimate(flops=3 << 20, bytes_accessed=(count + 1) << 20, transcendentals=0),
    )(*slabs)


def spread(pieces, second):
    return [pieces[0]] + [turn(pieces[step], step, second) for step in (1, 3, 2)]


def add_up(pieces):
    return sum(piece.astype(F32) for piece in pieces)


def body(images, variances, kernels, coefficients, intersections, offsets):
    core = lax.rem(lax.axis_index("visit"), 2)
    stays, plus, minus, swaps, swap_plus, swap_minus = match_tiles(
        jnp.transpose(intersections[0]),
        jnp.transpose(offsets[0], (1, 2, 0)),
        jnp.transpose(kernels[0], (1, 0, 2)),
        jnp.transpose(coefficients[0], (1, 0, 2)),
        images[0],
        variances[0],
    )
    swapped = across_core(swaps)
    below, above = across_z(plus, 1), across_z(minus, 3)
    opposite = opposite_frame([stays, swapped])
    summed = add_up(spread(sum_slabs(spread(opposite, False)), True)).astype(BF16)
    passed = across_z(summed, 2)
    below_too = across_both(lax.optimization_barrier((swap_plus, below, opposite[0]))[0], 1)
    above_too = across_both(lax.optimization_barrier((swap_minus, above, opposite[0]))[0], 3)
    begun = start_frame([stays, swapped, below, above])
    own = finish_frame(begun, [below_too, above_too], summed)
    pieces = sum_slabs(spread(own, False))
    rows = add_up(spread(pieces, True) + [passed])
    keep, got = rows[:STRIP], across_core(rows[STRIP:])
    numer = jnp.where(core == 0, keep, got)
    weight = jnp.where(core == 0, got, keep)
    return (numer / (weight + 1.0))[None], weight[None]


def solution(mesh):
    return jax.shard_map(
        body,
        mesh=mesh,
        in_specs=(
            P("visit", "patch", None, None),
            P("visit", "patch", None, None),
            P("visit", None, None, None),
            P("visit", "patch", None, None),
            P("visit", "patch", None),
            P("visit", "patch", None, None),
        ),
        out_specs=(P("patch", "visit", None), P("patch", "visit", None)),
        check_vma=False,
    )
```

```python
import functools

import jax
import jax.numpy as jnp
from jax import lax
from jax.experimental import pallas as pl
from jax.experimental.pallas import tpu as pltpu
from jax.sharding import PartitionSpec as P

TAPS = 31
BASES = 3
TILE = 512
PATCH_PIX = 1536
STRIP = 48
LANES = 128
ROWS = 8
SLAB = 384
WINDOWS = ((0, 0), (1, 64), (1, 192), (2, 256))
BF16 = jnp.bfloat16
F32 = jnp.float32


def visit_of(y, x, c):
    return (y * 4 + x) * 2 + c


def chips():
    return [(y, x) for y in range(4) for x in range(4)]


def turn(value, step, second):
    pairs = []
    for y, x in chips():
        for c in range(2):
            along_y = (c == 1) != second
            target = visit_of((y + step) % 4, x, c) if along_y else visit_of(y, (x + step) % 4, c)
            pairs.append((visit_of(y, x, c), target))
    return lax.ppermute(value, "visit", pairs)


def across_z(value, step):
    return lax.ppermute(value, "patch", [(z, (z + step) % 4) for z in range(4)])


def across_core(value):
    pairs = [(visit_of(y, x, c), visit_of(y, x, 1 - c)) for y, x in chips() for c in range(2)]
    return lax.ppermute(value, "visit", pairs)


def across_both(value, step):
    pairs = [
        (visit_of(y, x, c) * 4 + z, visit_of(y, x, 1 - c) * 4 + (z + step) % 4)
        for y, x in chips()
        for c in range(2)
        for z in range(4)
    ]
    return lax.ppermute(value, ("visit", "patch"), pairs)


def position():
    visit = lax.axis_index("visit")
    return lax.div(visit, 8), lax.rem(lax.div(visit, 2), 4), lax.rem(visit, 2), lax.axis_index("patch")


def lane_values(shape, pairs, default):
    lane = lax.broadcasted_iota(jnp.int32, shape, len(shape) - 1)
    out = jnp.full(shape, default, F32)
    for where, value in pairs:
        out = jnp.where(lane == where, value, out)
    return out


def match_kernel(
    patches_in, corners_in, taps_in, coeffs_in, images_in, variances_in, stays, plus, minus, swaps, swap_plus, swap_minus,
    patches, corners, taps, coeffs, images, variances, across, down, lanes, factors, numer, weight,
    in_sems, tile_sems, sems, wsems,
):
    tile = pl.program_id(0)
    loads = [
        [
            pltpu.make_async_copy(images_in.at[index], images.at[index], tile_sems.at[0, index]),
            pltpu.make_async_copy(variances_in.at[index], variances.at[index], tile_sems.at[1, index]),
        ]
        for index in (0, 1, 2, 3, tile)
    ]
    _, _, core, z = position()

    @pl.when(tile == 0)
    def _():
        small = [(patches_in, patches), (corners_in, corners), (taps_in, taps), (coeffs_in, coeffs)]
        copies = [pltpu.make_async_copy(a, b, in_sems.at[k]) for k, (a, b) in enumerate(small)]
        for copy in copies:
            copy.start()
        for pair in loads[:4]:
            for copy in pair:
                copy.start()
        for copy in copies:
            copy.wait()
        lanes[...] = jnp.zeros_like(lanes)
        for basis in range(BASES):
            factors[basis, 0:4, 0:3] = coeffs[basis].astype(F32)
            for axis in range(2):
                lanes[2 * basis + axis : 2 * basis + axis + 1, 0:TAPS] = taps[basis, axis : axis + 1, :].astype(F32)
        for basis in range(BASES):
            for axis in range(2):
                row = jnp.broadcast_to(lanes[2 * basis + axis : 2 * basis + axis + 1, :], (LANES, 3 * LANES))
                band = pltpu.roll(row, LANES - TAPS // 2, axis=1, stride=1, stride_axis=0)
                if axis == 0:
                    centred = pltpu.roll(row, LANES // 2 - TAPS // 2, axis=1, stride=1, stride_axis=0)
                    down[basis, 0] = band[:, LANES:].astype(BF16)
                    down[basis, 1] = centred[:, : 2 * LANES].astype(BF16)
                    down[basis, 2] = band[:, : 2 * LANES].astype(BF16)
                    continue
                band = band.T.astype(BF16)
                across[basis] = jnp.zeros((TILE, TILE), BF16)
                for block in range(TILE // LANES):
                    first = (block - 1) * LANES
                    low, high = max(first, 0), min(first + 3 * LANES, TILE)
                    span = slice(block * LANES, (block + 1) * LANES)
                    across[basis, low:high, span] = band[low - first : high - first, :]

    rows = lax.broadcasted_iota(jnp.int32, (TILE, 1), 0).astype(F32)
    columns = lax.broadcasted_iota(jnp.int32, (1, TILE), 1).astype(F32)
    rows = (rows - (TILE - 1) / 2.0) / (TILE / 2.0)
    columns = (columns - (TILE - 1) / 2.0) / (TILE / 2.0)
    for copy in loads[4]:
        copy.wait()
    total = jnp.zeros((TILE, TILE), F32)
    for basis in range(BASES):
        middle = jnp.dot(images[tile], across[basis], preferred_element_type=F32).astype(BF16)
        smoothed = jnp.concatenate(
            [
                jnp.dot(down[basis, kind], middle[first : first + 2 * LANES], preferred_element_type=F32)
                for kind, first in WINDOWS
            ],
            axis=0,
        )
        c0, c1, c2 = (factors[basis, pl.ds(tile, 1), k : k + 1] for k in range(3))
        total += ((c0 + c1 * columns) + c2 * rows) * smoothed
    inverse = 1.0 / variances[tile].astype(F32)
    numer[tile, 0:TILE] = (inverse * total).astype(BF16)
    weight[tile, 0:TILE] = inverse.astype(BF16)
    named, tops, lefts = [], [], []
    for which in range(2):
        patch = patches[which, tile].astype(F32)
        named += [(8 * which, patch), (8 * which + 1, patch)]
        for axis, parts in enumerate((tops, lefts)):
            corner = corners[which, axis, tile]
            fine = lax.rem(corner, 32)
            parts += [(8 * which, (corner - fine).astype(F32)), (8 * which + 1, fine.astype(F32))]
    for held in (numer, weight):
        for part, pairs in enumerate((named, tops, lefts)):
            note = lane_values((16, LANES), pairs, -1.0 if part == 0 else 0.0)
            held[tile, TILE : TILE + 16, part * LANES : (part + 1) * LANES] = note.astype(BF16)

    def each(index, act):
        for which in range(2):
            patch = patches[which, index]
            rank = jnp.int32(0)
            for other in range(8):
                before = (2 * index + which > other) & (patches[other % 2, other // 2] == patch)
                rank += jnp.where(before, 1, 0)
            rank = jnp.minimum(rank, 1)
            towards = lax.rem(patch - z + 4, 4)
            held, sent = numer.at[index], weight.at[index]
            sem, wsem = sems.at[index, which], wsems.at[index, which]
            for wanted, keep, give in (
                (0, stays.at[0], swaps.at[0]),
                (1, plus, swap_plus),
                (2, stays.at[1], swaps.at[1]),
                (3, minus, swap_minus),
            ):
                for own_core in range(2):

                    @pl.when((towards == wanted) & (core == own_core))
                    def _():
                        act(pltpu.make_async_copy(held, (give if own_core else keep).at[rank], sem))
                        act(pltpu.make_async_copy(sent, (keep if own_core else give).at[rank], wsem))

    each(tile, lambda copy: copy.start())

    @pl.when(tile == 3)
    def _():
        for index in range(4):
            each(index, lambda copy: copy.wait())


def match_tiles(patches, corners, taps, coeffs, images, variances):
    pair = jax.ShapeDtypeStruct((2, TILE + 16, TILE), BF16)
    quad = jax.ShapeDtypeStruct((2, 2, TILE + 16, TILE), BF16)
    return pl.pallas_call(
        match_kernel,
        grid=(4,),
        in_specs=[pl.BlockSpec(memory_space=pltpu.HBM)] * 6,
        out_specs=[pl.BlockSpec(memory_space=pl.ANY)] * 6,
        out_shape=[quad, pair, pair, quad, pair, pair],
        scratch_shapes=[
            pltpu.SMEM((2, 4), jnp.int32),
            pltpu.SMEM((2, 2, 4), jnp.int32),
            pltpu.VMEM((BASES, 2, TAPS), BF16),
            pltpu.VMEM((BASES, 4, 3), BF16),
            pltpu.VMEM((4, TILE, TILE), BF16),
            pltpu.VMEM((4, TILE, TILE), BF16),
            pltpu.VMEM((BASES, TILE, TILE), BF16),
            pltpu.VMEM((BASES, 3, LANES, 2 * LANES), BF16),
            pltpu.VMEM((8, 3 * LANES), F32),
            pltpu.VMEM((BASES, 8, LANES), F32),
            pltpu.VMEM((4, TILE + 16, TILE), BF16),
            pltpu.VMEM((4, TILE + 16, TILE), BF16),
            pltpu.SemaphoreType.DMA((4,)),
            pltpu.SemaphoreType.DMA((2, 4)),
            pltpu.SemaphoreType.DMA((4, 2)),
            pltpu.SemaphoreType.DMA((4, 2)),
        ],
        compiler_params=pltpu.CompilerParams(vmem_limit_bytes=60 << 20),
        cost_estimate=pl.CostEstimate(flops=6 << 30, bytes_accessed=12 << 20, transcendentals=0),
    )(patches, corners, taps, coeffs, images, variances)


def start_kernel(*refs):
    stacks, frame = refs[:-1], refs[-1]
    frame[...] = jnp.zeros_like(frame)
    add_tiles(0, stacks, frame)


def finish_kernel(count, *refs):
    frame, stacks, outs = refs[0], refs[1 : 1 + count], refs[-5:-1]
    add_tiles(0, stacks, frame)
    pack(frame, outs)


def opposite_kernel(*refs):
    stacks, outs, frame = refs[:-5], refs[-5:-1], refs[-1]
    frame[...] = jnp.zeros_like(frame)
    add_tiles(1, stacks, frame)
    pack(frame, outs)


def add_tiles(far, stacks, frame):
    patch = lax.rem(lax.axis_index("patch") + 2 * far, 4).astype(F32)
    inner = lax.broadcasted_iota(jnp.int32, (1, ROWS, LANES), 1)
    lane = lax.broadcasted_iota(jnp.int32, (1, ROWS, LANES), 2)
    groups = TILE // ROWS

    def add(tile):
        named, tops, lefts = (
            tile[TILE : TILE + 16, part * LANES : (part + 1) * LANES].astype(F32)[0:1] for part in range(3)
        )
        top = jnp.sum(jnp.where(named == patch, tops, 0.0)).astype(jnp.int32)
        left = jnp.sum(jnp.where(named == patch, lefts, 0.0)).astype(jnp.int32)
        first = jnp.minimum(lax.div(left, LANES) * LANES, PATCH_PIX - TILE - LANES)
        shift = left - first
        group, lead = lax.div(top, ROWS), lax.rem(top, ROWS)
        before = jnp.zeros((groups, ROWS, LANES), F32)
        for block in range(5):
            turned = jnp.zeros((groups, ROWS, LANES), F32)
            if block < 4:
                part = tile[0:TILE, block * LANES : (block + 1) * LANES].astype(F32)
                turned = pltpu.roll(part, shift, axis=1).reshape(groups, ROWS, LANES)
                turned = pltpu.roll(turned, lead, axis=1)
            moved = jnp.where(lane >= shift, turned, before)
            before = turned
            nothing = jnp.zeros((1, ROWS, LANES), F32)
            lower = jnp.concatenate([moved, nothing], axis=0)
            upper = jnp.concatenate([nothing, moved], axis=0)
            where = (
                pl.ds(group, groups + 1),
                slice(None),
                pl.ds(pl.multiple_of(first + block * LANES, LANES), LANES),
            )
            frame[where] += jnp.where(inner >= lead, lower, upper)

    for stack in stacks:

        def both(slot, carry, stack=stack):
            add(stack.at[far, slot] if len(stack.shape) == 4 else stack.at[slot])
            return carry

        lax.fori_loop(0, 2, both, 0)


def pack(frame, outs):
    y, x, core, _ = position()
    for out in range(4):
        for part in range(4):
            dx, dy = jnp.where(core == 0, out, part), jnp.where(core == 0, part, out)
            for dc in range(2):
                row = 8 * STRIP * lax.rem(y + dy, 4) + 2 * STRIP * lax.rem(x + dx, 4) + STRIP * lax.rem(core + dc, 2)
                strip = frame[pl.ds(lax.div(row, ROWS), STRIP // ROWS)]
                at = (2 * part + dc) * STRIP
                outs[out][at : at + STRIP, :] = strip.reshape(STRIP, PATCH_PIX).astype(BF16)


SLABS = [jax.ShapeDtypeStruct((SLAB, PATCH_PIX), BF16)] * 4
FRAME = (PATCH_PIX // ROWS + 1, ROWS, PATCH_PIX)


def frame_options(tiles, grant):
    cost = pl.CostEstimate(flops=tiles << 29, bytes_accessed=(5 + tiles) << 20, transcendentals=0)
    return dict(compiler_params=pltpu.CompilerParams(vmem_limit_bytes=grant << 20), cost_estimate=cost)


def opposite_frame(stacks):
    return pl.pallas_call(
        opposite_kernel, out_shape=SLABS, scratch_shapes=[pltpu.VMEM(FRAME, F32)], **frame_options(4, 22)
    )(*stacks)


def start_frame(stacks):
    return pl.pallas_call(start_kernel, out_shape=jax.ShapeDtypeStruct(FRAME, F32), **frame_options(8, 20))(*stacks)


def finish_frame(frame, stacks, after):
    spaces = [pltpu.VMEM] * (1 + len(stacks)) + [pl.ANY]
    return pl.pallas_call(
        functools.partial(finish_kernel, len(stacks)),
        in_specs=[pl.BlockSpec(memory_space=space) for space in spaces],
        out_shape=SLABS + [jax.ShapeDtypeStruct(FRAME, F32)],
        input_output_aliases={0: 4},
        **frame_options(4, 30),
    )(frame, *stacks, after)[:4]


def sum_kernel(count, *refs):
    for part in range(4):
        rows = slice(part * 2 * STRIP, (part + 1) * 2 * STRIP)
        total = refs[0][rows].astype(F32)
        for ref in refs[1:count]:
            total += ref[rows].astype(F32)
        refs[count + part][...] = total.astype(BF16)


def sum_slabs(slabs):
    count = len(slabs)
    out = jax.ShapeDtypeStruct((2 * STRIP, PATCH_PIX), BF16)
    return pl.pallas_call(
        functools.partial(sum_kernel, count),
        out_shape=[out] * 4,
        compiler_params=pltpu.CompilerParams(vmem_limit_bytes=12 << 20),
        cost_estimate=pl.CostEstimate(flops=3 << 20, bytes_accessed=(count + 1) << 20, transcendentals=0),
    )(*slabs)


def spread(pieces, second):
    return [pieces[0]] + [turn(pieces[step], step, second) for step in (2, 1, 3)]


def add_up(pieces):
    return sum(piece.astype(F32) for piece in pieces)


def body(images, variances, kernels, coefficients, intersections, offsets):
    core = lax.rem(lax.axis_index("visit"), 2)
    stays, plus, minus, swaps, swap_plus, swap_minus = match_tiles(
        jnp.transpose(intersections[0]),
        jnp.transpose(offsets[0], (1, 2, 0)),
        jnp.transpose(kernels[0], (1, 0, 2)),
        jnp.transpose(coefficients[0], (1, 0, 2)),
        images[0],
        variances[0],
    )
    swapped = across_core(swaps)
    below, above = across_z(plus, 1), across_z(minus, 3)
    opposite = opposite_frame([stays, swapped])
    summed = add_up(spread(sum_slabs(spread(opposite, False)), True)).astype(BF16)
    passed = across_z(summed, 2)
    below_too = across_both(lax.optimization_barrier((swap_plus, below, opposite[0]))[0], 1)
    above_too = across_both(lax.optimization_barrier((swap_minus, above, opposite[0]))[0], 3)
    begun = start_frame([stays, swapped, below, above])
    own = finish_frame(begun, [below_too, above_too], summed)
    pieces = sum_slabs(spread(own, False))
    rows = add_up(spread(pieces, True) + [passed])
    keep, got = rows[:STRIP], across_core(rows[STRIP:])
    numer = jnp.where(core == 0, keep, got)
    weight = jnp.where(core == 0, got, keep)
    return (numer / (weight + 1.0))[None], weight[None]


def solution(mesh):
    return jax.shard_map(
        body,
        mesh=mesh,
        in_specs=(
            P("visit", "patch", None, None),
            P("visit", "patch", None, None),
            P("visit", None, None, None),
            P("visit", "patch", None, None),
            P("visit", "patch", None),
            P("visit", "patch", None, None),
        ),
        out_specs=(P("patch", "visit", None), P("patch", "visit", None)),
        check_vma=False,
    )
```

```python
import functools

import jax
import jax.numpy as jnp
from jax import lax
from jax.experimental import pallas as pl
from jax.experimental.pallas import tpu as pltpu
from jax.sharding import PartitionSpec as P

TAPS = 31
BASES = 3
TILE = 512
PATCH_PIX = 1536
STRIP = 48
LANES = 128
ROWS = 8
SLAB = 384
WINDOWS = ((0, 0), (1, 64), (1, 192), (2, 256))
BF16 = jnp.bfloat16
F32 = jnp.float32


def visit_of(y, x, c):
    return (y * 4 + x) * 2 + c


def chips():
    return [(y, x) for y in range(4) for x in range(4)]


def turn(value, step, second):
    pairs = []
    for y, x in chips():
        for c in range(2):
            along_y = (c == 1) != second
            target = visit_of((y + step) % 4, x, c) if along_y else visit_of(y, (x + step) % 4, c)
            pairs.append((visit_of(y, x, c), target))
    return lax.ppermute(value, "visit", pairs)


def across_z(value, step):
    return lax.ppermute(value, "patch", [(z, (z + step) % 4) for z in range(4)])


def across_core(value):
    pairs = [(visit_of(y, x, c), visit_of(y, x, 1 - c)) for y, x in chips() for c in range(2)]
    return lax.ppermute(value, "visit", pairs)


def across_both(value, step):
    pairs = [
        (visit_of(y, x, c) * 4 + z, visit_of(y, x, 1 - c) * 4 + (z + step) % 4)
        for y, x in chips()
        for c in range(2)
        for z in range(4)
    ]
    return lax.ppermute(value, ("visit", "patch"), pairs)


def position():
    visit = lax.axis_index("visit")
    return lax.div(visit, 8), lax.rem(lax.div(visit, 2), 4), lax.rem(visit, 2), lax.axis_index("patch")


def lane_values(shape, pairs, default):
    lane = lax.broadcasted_iota(jnp.int32, shape, len(shape) - 1)
    out = jnp.full(shape, default, F32)
    for where, value in pairs:
        out = jnp.where(lane == where, value, out)
    return out


def match_kernel(
    patches_in, corners_in, taps_in, coeffs_in, images_in, variances_in, stays, plus, minus, swaps, swap_plus, swap_minus,
    patches, corners, taps, coeffs, images, variances, across, down, lanes, factors, numer, weight,
    in_sems, tile_sems, sems, wsems,
):
    tile = pl.program_id(0)
    loads = [
        [
            pltpu.make_async_copy(images_in.at[index], images.at[index], tile_sems.at[0, index]),
            pltpu.make_async_copy(variances_in.at[index], variances.at[index], tile_sems.at[1, index]),
        ]
        for index in (0, 1, 2, 3, tile)
    ]
    _, _, core, z = position()

    @pl.when(tile == 0)
    def _():
        small = [(patches_in, patches), (corners_in, corners), (taps_in, taps), (coeffs_in, coeffs)]
        copies = [pltpu.make_async_copy(a, b, in_sems.at[k]) for k, (a, b) in enumerate(small)]
        for copy in copies:
            copy.start()
        for pair in loads[:4]:
            for copy in pair:
                copy.start()
        for copy in copies:
            copy.wait()
        lanes[...] = jnp.zeros_like(lanes)
        for basis in range(BASES):
            factors[basis, 0:4, 0:3] = coeffs[basis].astype(F32)
            for axis in range(2):
                lanes[2 * basis + axis : 2 * basis + axis + 1, 0:TAPS] = taps[basis, axis : axis + 1, :].astype(F32)
        for basis in range(BASES):
            for axis in range(2):
                row = jnp.broadcast_to(lanes[2 * basis + axis : 2 * basis + axis + 1, :], (LANES, 3 * LANES))
                band = pltpu.roll(row, LANES - TAPS // 2, axis=1, stride=1, stride_axis=0)
                if axis == 0:
                    centred = pltpu.roll(row, LANES // 2 - TAPS // 2, axis=1, stride=1, stride_axis=0)
                    down[basis, 0] = band[:, LANES:].astype(BF16)
                    down[basis, 1] = centred[:, : 2 * LANES].astype(BF16)
                    down[basis, 2] = band[:, : 2 * LANES].astype(BF16)
                    continue
                band = band.T.astype(BF16)
                across[:, basis * TILE : (basis + 1) * TILE] = jnp.zeros((TILE, TILE), BF16)
                for block in range(TILE // LANES):
                    first = (block - 1) * LANES
                    low, high = max(first, 0), min(first + 3 * LANES, TILE)
                    at = basis * TILE + block * LANES
                    across[low:high, at : at + LANES] = band[low - first : high - first, :]

    rows = lax.broadcasted_iota(jnp.int32, (TILE, 1), 0).astype(F32)
    columns = lax.broadcasted_iota(jnp.int32, (1, TILE), 1).astype(F32)
    rows = (rows - (TILE - 1) / 2.0) / (TILE / 2.0)
    columns = (columns - (TILE - 1) / 2.0) / (TILE / 2.0)
    for copy in loads[4]:
        copy.wait()
    middles = jnp.dot(images[tile], across[...], preferred_element_type=F32).astype(BF16)
    total = jnp.zeros((TILE, TILE), F32)
    for basis in range(BASES):
        middle = middles[:, basis * TILE : (basis + 1) * TILE]
        smoothed = jnp.concatenate(
            [
                jnp.dot(down[basis, kind], middle[first : first + 2 * LANES], preferred_element_type=F32)
                for kind, first in WINDOWS
            ],
            axis=0,
        )
        c0, c1, c2 = (factors[basis, pl.ds(tile, 1), k : k + 1] for k in range(3))
        total += ((c0 + c1 * columns) + c2 * rows) * smoothed
    inverse = 1.0 / variances[tile].astype(F32)
    numer[tile, 0:TILE] = (inverse * total).astype(BF16)
    weight[tile, 0:TILE] = inverse.astype(BF16)
    named, tops, lefts = [], [], []
    for which in range(2):
        patch = patches[which, tile].astype(F32)
        named += [(8 * which, patch), (8 * which + 1, patch)]
        for axis, parts in enumerate((tops, lefts)):
            corner = corners[which, axis, tile]
            fine = lax.rem(corner, 32)
            parts += [(8 * which, (corner - fine).astype(F32)), (8 * which + 1, fine.astype(F32))]
    for held in (numer, weight):
        for part, pairs in enumerate((named, tops, lefts)):
            note = lane_values((16, LANES), pairs, -1.0 if part == 0 else 0.0)
            held[tile, TILE : TILE + 16, part * LANES : (part + 1) * LANES] = note.astype(BF16)

    def each(index, act):
        for which in range(2):
            patch = patches[which, index]
            rank = jnp.int32(0)
            for other in range(8):
                before = (2 * index + which > other) & (patches[other % 2, other // 2] == patch)
                rank += jnp.where(before, 1, 0)
            rank = jnp.minimum(rank, 1)
            towards = lax.rem(patch - z + 4, 4)
            held, sent = numer.at[index], weight.at[index]
            sem, wsem = sems.at[index, which], wsems.at[index, which]
            for wanted, keep, give in (
                (0, stays.at[0], swaps.at[0]),
                (1, plus, swap_plus),
                (2, stays.at[1], swaps.at[1]),
                (3, minus, swap_minus),
            ):
                for own_core in range(2):

                    @pl.when((towards == wanted) & (core == own_core))
                    def _():
                        act(pltpu.make_async_copy(held, (give if own_core else keep).at[rank], sem))
                        act(pltpu.make_async_copy(sent, (keep if own_core else give).at[rank], wsem))

    each(tile, lambda copy: copy.start())

    @pl.when(tile == 3)
    def _():
        for index in range(4):
            each(index, lambda copy: copy.wait())


def match_tiles(patches, corners, taps, coeffs, images, variances):
    pair = jax.ShapeDtypeStruct((2, TILE + 16, TILE), BF16)
    quad = jax.ShapeDtypeStruct((2, 2, TILE + 16, TILE), BF16)
    return pl.pallas_call(
        match_kernel,
        grid=(4,),
        in_specs=[pl.BlockSpec(memory_space=pltpu.HBM)] * 6,
        out_specs=[pl.BlockSpec(memory_space=pl.ANY)] * 6,
        out_shape=[quad, pair, pair, quad, pair, pair],
        scratch_shapes=[
            pltpu.SMEM((2, 4), jnp.int32),
            pltpu.SMEM((2, 2, 4), jnp.int32),
            pltpu.VMEM((BASES, 2, TAPS), BF16),
            pltpu.VMEM((BASES, 4, 3), BF16),
            pltpu.VMEM((4, TILE, TILE), BF16),
            pltpu.VMEM((4, TILE, TILE), BF16),
            pltpu.VMEM((TILE, BASES * TILE), BF16),
            pltpu.VMEM((BASES, 3, LANES, 2 * LANES), BF16),
            pltpu.VMEM((8, 3 * LANES), F32),
            pltpu.VMEM((BASES, 8, LANES), F32),
            pltpu.VMEM((4, TILE + 16, TILE), BF16),
            pltpu.VMEM((4, TILE + 16, TILE), BF16),
            pltpu.SemaphoreType.DMA((4,)),
            pltpu.SemaphoreType.DMA((2, 4)),
            pltpu.SemaphoreType.DMA((4, 2)),
            pltpu.SemaphoreType.DMA((4, 2)),
        ],
        compiler_params=pltpu.CompilerParams(vmem_limit_bytes=60 << 20),
        cost_estimate=pl.CostEstimate(flops=6 << 30, bytes_accessed=12 << 20, transcendentals=0),
    )(patches, corners, taps, coeffs, images, variances)


def start_kernel(*refs):
    stacks, frame = refs[:-1], refs[-1]
    frame[...] = jnp.zeros_like(frame)
    add_tiles(0, stacks, frame)


def finish_kernel(count, *refs):
    frame, stacks, outs = refs[0], refs[1 : 1 + count], refs[-5:-1]
    add_tiles(0, stacks, frame)
    pack(frame, outs)


def opposite_kernel(*refs):
    stacks, outs, frame = refs[:-5], refs[-5:-1], refs[-1]
    frame[...] = jnp.zeros_like(frame)
    add_tiles(1, stacks, frame)
    pack(frame, outs)


def add_tiles(far, stacks, frame):
    patch = lax.rem(lax.axis_index("patch") + 2 * far, 4).astype(F32)
    inner = lax.broadcasted_iota(jnp.int32, (1, ROWS, LANES), 1)
    lane = lax.broadcasted_iota(jnp.int32, (1, ROWS, LANES), 2)
    groups = TILE // ROWS

    def add(tile):
        named, tops, lefts = (
            tile[TILE : TILE + 16, part * LANES : (part + 1) * LANES].astype(F32)[0:1] for part in range(3)
        )
        top = jnp.sum(jnp.where(named == patch, tops, 0.0)).astype(jnp.int32)
        left = jnp.sum(jnp.where(named == patch, lefts, 0.0)).astype(jnp.int32)
        first = jnp.minimum(lax.div(left, LANES) * LANES, PATCH_PIX - TILE - LANES)
        shift = left - first
        group, lead = lax.div(top, ROWS), lax.rem(top, ROWS)
        before = jnp.zeros((groups, ROWS, LANES), F32)
        for block in range(5):
            turned = jnp.zeros((groups, ROWS, LANES), F32)
            if block < 4:
                part = tile[0:TILE, block * LANES : (block + 1) * LANES].astype(F32)
                turned = pltpu.roll(part, shift, axis=1).reshape(groups, ROWS, LANES)
                turned = pltpu.roll(turned, lead, axis=1)
            moved = jnp.where(lane >= shift, turned, before)
            before = turned
            nothing = jnp.zeros((1, ROWS, LANES), F32)
            lower = jnp.concatenate([moved, nothing], axis=0)
            upper = jnp.concatenate([nothing, moved], axis=0)
            where = (
                pl.ds(group, groups + 1),
                slice(None),
                pl.ds(pl.multiple_of(first + block * LANES, LANES), LANES),
            )
            frame[where] += jnp.where(inner >= lead, lower, upper)

    for stack in stacks:

        def both(slot, carry, stack=stack):
            add(stack.at[far, slot] if len(stack.shape) == 4 else stack.at[slot])
            return carry

        lax.fori_loop(0, 2, both, 0)


def pack(frame, outs):
    y, x, core, _ = position()
    for out in range(4):
        for part in range(4):
            dx, dy = jnp.where(core == 0, out, part), jnp.where(core == 0, part, out)
            for dc in range(2):
                row = 8 * STRIP * lax.rem(y + dy, 4) + 2 * STRIP * lax.rem(x + dx, 4) + STRIP * lax.rem(core + dc, 2)
                strip = frame[pl.ds(lax.div(row, ROWS), STRIP // ROWS)]
                at = (2 * part + dc) * STRIP
                outs[out][at : at + STRIP, :] = strip.reshape(STRIP, PATCH_PIX).astype(BF16)


SLABS = [jax.ShapeDtypeStruct((SLAB, PATCH_PIX), BF16)] * 4
FRAME = (PATCH_PIX // ROWS + 1, ROWS, PATCH_PIX)


def frame_options(tiles, grant):
    cost = pl.CostEstimate(flops=tiles << 29, bytes_accessed=(5 + tiles) << 20, transcendentals=0)
    return dict(compiler_params=pltpu.CompilerParams(vmem_limit_bytes=grant << 20), cost_estimate=cost)


def opposite_frame(stacks):
    return pl.pallas_call(
        opposite_kernel, out_shape=SLABS, scratch_shapes=[pltpu.VMEM(FRAME, F32)], **frame_options(4, 22)
    )(*stacks)


def start_frame(stacks):
    return pl.pallas_call(start_kernel, out_shape=jax.ShapeDtypeStruct(FRAME, F32), **frame_options(8, 20))(*stacks)


def finish_frame(frame, stacks, after):
    spaces = [pltpu.VMEM] * (1 + len(stacks)) + [pl.ANY]
    return pl.pallas_call(
        functools.partial(finish_kernel, len(stacks)),
        in_specs=[pl.BlockSpec(memory_space=space) for space in spaces],
        out_shape=SLABS + [jax.ShapeDtypeStruct(FRAME, F32)],
        input_output_aliases={0: 4},
        **frame_options(4, 30),
    )(frame, *stacks, after)[:4]


def sum_kernel(count, *refs):
    for part in range(4):
        rows = slice(part * 2 * STRIP, (part + 1) * 2 * STRIP)
        total = refs[0][rows].astype(F32)
        for ref in refs[1:count]:
            total += ref[rows].astype(F32)
        refs[count + part][...] = total.astype(BF16)


def sum_slabs(slabs):
    count = len(slabs)
    out = jax.ShapeDtypeStruct((2 * STRIP, PATCH_PIX), BF16)
    return pl.pallas_call(
        functools.partial(sum_kernel, count),
        out_shape=[out] * 4,
        compiler_params=pltpu.CompilerParams(vmem_limit_bytes=12 << 20),
        cost_estimate=pl.CostEstimate(flops=3 << 20, bytes_accessed=(count + 1) << 20, transcendentals=0),
    )(*slabs)


def spread(pieces, second):
    return [pieces[0]] + [turn(pieces[step], step, second) for step in (2, 1, 3)]


def add_up(pieces):
    return sum(piece.astype(F32) for piece in pieces)


def body(images, variances, kernels, coefficients, intersections, offsets):
    core = lax.rem(lax.axis_index("visit"), 2)
    stays, plus, minus, swaps, swap_plus, swap_minus = match_tiles(
        jnp.transpose(intersections[0]),
        jnp.transpose(offsets[0], (1, 2, 0)),
        jnp.transpose(kernels[0], (1, 0, 2)),
        jnp.transpose(coefficients[0], (1, 0, 2)),
        images[0],
        variances[0],
    )
    swapped = across_core(swaps)
    below, above = across_z(plus, 1), across_z(minus, 3)
    opposite = opposite_frame([stays, swapped])
    summed = add_up(spread(sum_slabs(spread(opposite, False)), True)).astype(BF16)
    passed = across_z(summed, 2)
    below_too = across_both(lax.optimization_barrier((swap_plus, below, opposite[0]))[0], 1)
    above_too = across_both(lax.optimization_barrier((swap_minus, above, opposite[0]))[0], 3)
    begun = start_frame([stays, swapped, below, above])
    own = finish_frame(begun, [below_too, above_too], summed)
    pieces = sum_slabs(spread(own, False))
    rows = add_up(spread(pieces, True) + [passed])
    keep, got = rows[:STRIP], across_core(rows[STRIP:])
    numer = jnp.where(core == 0, keep, got)
    weight = jnp.where(core == 0, got, keep)
    return (numer / (weight + 1.0))[None], weight[None]


def solution(mesh):
    return jax.shard_map(
        body,
        mesh=mesh,
        in_specs=(
            P("visit", "patch", None, None),
            P("visit", "patch", None, None),
            P("visit", None, None, None),
            P("visit", "patch", None, None),
            P("visit", "patch", None),
            P("visit", "patch", None, None),
        ),
        out_specs=(P("patch", "visit", None), P("patch", "visit", None)),
        check_vma=False,
    )
```
